512 devices in a mesh: dp: 64 (over y, z), mp: 8 (over x, core).
Axes of the slice: x: 4, y: 4, z: 16, core: 2. Of those that a mesh axis runs over, the one named last changes fastest.
Arguments:
- hidden: bfloat16 [8192, 28672], P('dp', 'mp'), may hold values from -6 to 6
- cotangent: bfloat16 [8192, 8192], P('dp', 'mp'), may hold values from -6 to 6
- adapter_down: bfloat16 [28672, 64], P('mp'), may hold values from -0.03125 to 0.03125
- adapter_up: bfloat16 [64, 8192], P(None, 'mp'), may hold values from -0.75 to 0.75
- owner_per_block: int32 [8, 9], replicated, may hold values from 0 to 63, as said below
- left_statistics: float32 [128, 512, 512], P('dp'), as said below
- right_statistics: float32 [128, 64, 64], P('dp'), as said below
Outputs:
- update_a: bfloat16 [28672, 64], P('mp')
- update_b: bfloat16 [64, 8192], P(None, 'mp')
The draws below stay inside these ranges and needn't reach their ends.
Inputs may be any that keep to these rules, and one draw needn't show every extreme that they name: `owner_per_block`: entry [m, b] is the dp index that owns block b of model group m; over all groups together no index owns more than 2 blocks, and some index owns exactly 2. `left_statistics`: each [s] is a symmetric positive definite matrix, the statistic of the block that dp index s // 2 holds in its slot s % 2; slots that hold no block are not read. `right_statistics`: each [s] is a symmetric positive definite matrix, ordered as left_statistics.
All inputs are finite; a program needn't handle non-finite values.
Results may differ from the reference program's by a relative error of at most 0.0052.
Values may be sent and summed in bfloat16 or wider, within the bound.
A program may use at most 64 MiB of HBM per device.

```python
import math
import jax
import jax.numpy as jnp
from jax import lax

MODEL_WIDTH = 8192
FEEDFORWARD_UNITS = 28672
ADAPTER_RANK = 64
BW = 512
ITERS = 2
TOKEN_TOTAL = 8192
NB = 9
NBT = 72
CAP = 2
SLOTS = 128
N_DP = 64
N_MP = 8


def spd_stack(key, count, order, base, spread, rate_low, rate_high):
    keys = jax.random.split(key, count)
    positions = jnp.arange(order)
    distance = jnp.abs(positions[:, None] - positions[None, :]).astype(jnp.float32)
    identity = jnp.eye(order, dtype=jnp.float32)

    def one_matrix(entry_key):
        key_rate, key_angle, key_scale = jax.random.split(entry_key, 3)
        decay_rate = jax.random.uniform(key_rate, (), jnp.float32, rate_low, rate_high)
        angle = jax.random.uniform(key_angle, (order,), jnp.float32, -jnp.pi, jnp.pi)
        log_scale = jax.random.uniform(key_scale, (order,), jnp.float32, 0.0, spread)
        row_scale = jnp.exp(0.5 * log_scale)
        kernel = jnp.power(decay_rate, distance) * jnp.cos(angle[:, None] - angle[None, :]) + 0.5 * identity
        return base * row_scale[:, None] * row_scale[None, :] * kernel
    return lax.map(one_matrix, keys)


def draw_owner_per_block(key, part):
    key = jax.random.fold_in(key, 7)
    key_slots, key_blocks = jax.random.split(key)
    order_slots = jax.random.permutation(key_slots, SLOTS)
    position = jnp.argsort(order_slots)
    slot_ids = jnp.arange(SLOTS)
    half_owner = N_DP // 2
    score = jnp.where(slot_ids // CAP == half_owner, slot_ids % CAP - 2 * CAP, jnp.where((slot_ids == 0) | (slot_ids == CAP), -CAP, position))
    chosen = jnp.argsort(score)[:NBT]
    owners = (chosen // CAP).astype(jnp.int32)
    owners = owners[jax.random.permutation(key_blocks, NBT)]
    return owners.reshape(N_MP, NB).astype(jnp.int32)


def draw_left_statistics(key, part):
    key = jax.random.fold_in(key, 11)
    base = 0.2 * 4.0 * MODEL_WIDTH / TOKEN_TOTAL
    stack = spd_stack(key, SLOTS, BW, base, math.log(10.0), 0.8, 0.98)
    return stack


def draw_right_statistics(key, part):
    key = jax.random.fold_in(key, 13)
    base = 0.2 * 4.0 * MODEL_WIDTH * BW / (ADAPTER_RANK * TOKEN_TOTAL)
    stack = spd_stack(key, SLOTS, ADAPTER_RANK, base, math.log(10.0), 0.8, 0.98)
    return stack


def block_scale(key, shape, shards, low, top_value):
    gain = 1.0
    for axis_at, shards_of in shards:
        steps = jax.random.uniform(jax.random.fold_in(jax.random.fold_in(key, 6), axis_at), (shards_of,), jnp.float32, low / len(shards), top_value / len(shards))
        gain = gain * jnp.repeat(jnp.exp(steps), shape[axis_at] // shards_of).reshape((-1,) + (1,) * (len(shape) - 1 - axis_at))
    return gain


def noise(stream_key, extent, width, most, cuts=(), kind=jnp.bfloat16):
    entries = jax.random.normal(stream_key, extent, jnp.float32) * width
    if len(cuts) > 0:
        entries = block_scale(stream_key, extent, cuts, -0.22, 0.18) * entries
    return jnp.clip(entries, min=-most, max=most).astype(kind)


def setup_inputs(seed: int = 0) -> dict:
    key_list = jax.random.split(jax.random.key(seed), 8)
    hidden = noise(key_list[0], (TOKEN_TOTAL, FEEDFORWARD_UNITS), 1.0, 6.0, ((0, 64), (1, 8)))
    cotangent = noise(key_list[1], (TOKEN_TOTAL, MODEL_WIDTH), 1.0, 6.0, ((0, 64), (1, 8)))
    adapter_down = noise(key_list[2], (FEEDFORWARD_UNITS, ADAPTER_RANK), FEEDFORWARD_UNITS ** -0.5, 0.03125, ((0, 8),))
    adapter_up = noise(key_list[3], (ADAPTER_RANK, MODEL_WIDTH), ADAPTER_RANK ** -0.5, 0.75, ((1, 8),))
    owner_per_block = draw_owner_per_block(jax.random.fold_in(key_list[7], 71), 0)
    left_statistics = draw_left_statistics(jax.random.fold_in(key_list[7], 71), 0)
    right_statistics = draw_right_statistics(jax.random.fold_in(key_list[7], 71), 0)
    return dict(hidden=hidden, cotangent=cotangent, adapter_down=adapter_down, adapter_up=adapter_up, owner_per_block=owner_per_block, left_statistics=left_statistics, right_statistics=right_statistics)


ADAPTER_SCALE = 2.0
BETA_STAT = 0.9
EPS_NORM = 1e-06

def matmul_high(first, second):
    return jnp.matmul(first, second, precision=lax.Precision.HIGHEST)

def inverse_root(stat):
    matrix_size = stat.shape[-1]
    identity = jnp.eye(matrix_size, dtype=jnp.float32)
    frobenius = jnp.sqrt(lax.optimization_barrier(jnp.sum(stat * stat, axis=(-2, -1), keepdims=True)))
    z_scale = 5.0 / (2.0 * frobenius)
    mat_m = z_scale * stat
    mat_h = jnp.sqrt(jnp.sqrt(z_scale)) * identity
    for iteration in range(ITERS):
        mat_q = (5.0 * identity - mat_m) / 4.0
        mat_h = matmul_high(mat_h, mat_q)
        if iteration + 1 < ITERS:
            square = matmul_high(mat_q, mat_q)
            mat_m = matmul_high(matmul_high(square, square), mat_m)
    return mat_h

def precondition(block, left_prev, right_prev):
    block_t = jnp.swapaxes(block, -1, -2)
    left_stat = BETA_STAT * left_prev + (1.0 - BETA_STAT) * matmul_high(block, block_t)
    right_stat = BETA_STAT * right_prev + (1.0 - BETA_STAT) * matmul_high(block_t, block)
    precond = matmul_high(matmul_high(inverse_root(left_stat), block), inverse_root(right_stat))
    mean_square = lax.optimization_barrier(jnp.mean(precond * precond, axis=(-2, -1), keepdims=True))
    return precond * lax.rsqrt(mean_square + EPS_NORM)

def reference(hidden, cotangent, adapter_down, adapter_up, owner_per_block, left_statistics, right_statistics):
    inner_product = jnp.dot(hidden, adapter_down, preferred_element_type=jnp.float32).astype(jnp.bfloat16)
    outer_product = jnp.dot(cotangent, adapter_up.T, preferred_element_type=jnp.float32).astype(jnp.bfloat16)
    scale_factor = ADAPTER_SCALE / TOKEN_TOTAL
    grad_a = jnp.dot(hidden.T, outer_product, preferred_element_type=jnp.float32) * scale_factor
    grad_b = jnp.dot(cotangent.T, inner_product, preferred_element_type=jnp.float32) * scale_factor
    rows_first = FEEDFORWARD_UNITS // N_MP
    rows_second = MODEL_WIDTH // N_MP
    groups = jnp.concatenate([grad_a.reshape(N_MP, rows_first, ADAPTER_RANK), grad_b.reshape(N_MP, rows_second, ADAPTER_RANK)], axis=1)
    groups = groups.reshape(NBT, BW, ADAPTER_RANK)
    owners_flat = owner_per_block.reshape(-1).astype(jnp.int32)
    same_owner = owners_flat[:, None] == owners_flat[None, :]
    earlier = jnp.arange(NBT)[None, :] < jnp.arange(NBT)[:, None]
    slot_of = lax.optimization_barrier(jnp.sum((same_owner & earlier).astype(jnp.int32), axis=1)).astype(jnp.int32)
    slot_index = (owners_flat * CAP + slot_of).astype(jnp.int32)
    left_prev = jnp.take(left_statistics, slot_index, axis=0)
    right_prev = jnp.take(right_statistics, slot_index, axis=0)
    scaled = lax.map(lambda entry: precondition(entry[0], entry[1], entry[2]), (groups, left_prev, right_prev))
    scaled = scaled.astype(jnp.bfloat16).reshape(N_MP, NB * BW, ADAPTER_RANK)
    update_a = scaled[:, :rows_first].reshape(FEEDFORWARD_UNITS, ADAPTER_RANK)
    update_b = scaled[:, rows_first:].reshape(MODEL_WIDTH, ADAPTER_RANK).T
    return (update_a, update_b)
```

```python
import functools

import jax
import jax.numpy as jnp
from jax import lax
from jax.experimental import pallas as pl
from jax.experimental.pallas import tpu as pltpu
from jax.sharding import PartitionSpec as P

Z_EXTENT = 16
BLOCKS_PER_CHUNK = 4
LANES = 128

ADAPTER_SCALE = 2.0
BETA_STAT = 0.9
EPS_NORM = 1e-06
MESH = pl.DeviceIdType.MESH
BF16 = jnp.bfloat16
F32 = jnp.float32

NN = (((1,), (0,)), ((), ()))
NT = (((1,), (1,)), ((), ()))
TN = (((0,), (0,)), ((), ()))


def split(value):
    high = value.astype(BF16)
    return high, (value - high.astype(F32)).astype(BF16)


def dot3(first, second, dims):
    (fh, fl), (sh, sl) = first, second
    dot = functools.partial(lax.dot_general, dimension_numbers=dims, preferred_element_type=F32)
    return dot(fh, sh) + (dot(fl, sh) + dot(fh, sl))


def eye(n):
    return (
        lax.broadcasted_iota(jnp.int32, (n, n), 0) == lax.broadcasted_iota(jnp.int32, (n, n), 1)
    ).astype(F32)


def total(value):
    return jnp.sum(jnp.sum(value, axis=0, keepdims=True), axis=1, keepdims=True)


def precondition(block_t, left_prev, right_prev):
    rank = block_t.shape[0]
    halves = split(block_t)
    left = BETA_STAT * left_prev + (1.0 - BETA_STAT) * dot3(halves, halves, TN)
    right = BETA_STAT * right_prev + (1.0 - BETA_STAT) * dot3(halves, halves, NT)

    left_z = 5.0 / (2.0 * jnp.sqrt(total(left * left)))
    left_s = split(left)
    right_z = 5.0 / (2.0 * jnp.sqrt(total(right * right)))
    right_m = right_z * right
    right_s = split(right_m)

    def by_left(value):
        return dot3(split(value), left_s, NN) * left_z

    def by_right(value):
        return dot3(right_s, split(value), NN)

    moved = by_left(block_t)
    for _ in range(4):
        moved = (5.0 * moved - by_left(moved)) / 4.0
    out = (5.0 * block_t - moved) / 4.0
    out = jnp.sqrt(jnp.sqrt(left_z)) * ((5.0 * out - by_left(out)) / 4.0)

    moved = right_m
    for _ in range(4):
        moved = (5.0 * moved - by_right(moved)) / 4.0
    root = (5.0 * eye(rank) - moved) / 4.0
    root = jnp.sqrt(jnp.sqrt(right_z)) * ((5.0 * root - by_right(root)) / 4.0)

    out = dot3(split(root), split(out), NN)
    mean_square = total(out * out) / (out.shape[0] * out.shape[1])
    return out * lax.rsqrt(mean_square + EPS_NORM)


def kernel(
    cfg,
    tab, hid, cot, down, up, left_hbm, right_prev,
    out_a, out_b,
    part, a_recv, io, gsend, yrecv, zstage, zsend, zrecv, grow, mpbuf, dsend, drecv, left_buf,
    fsend, frecv, fb, fmp, fmpf, hrow, fin, finf,
    left_sem, s_a1, r_a1, s_a2, r_a2, s_y, r_y, s_z, r_z, s_d1, r_d1, s_d2, r_d2,
    s_f1, r_f1, s_f2, r_f2, s_fz, r_fz, s_fy, r_fy,
):
    n_dp, n_mp, ny, nz, rank, width, nb = cfg
    parts = width // LANES
    owners = n_dp // n_mp
    cap = 2
    tile = BLOCKS_PER_CHUNK * parts
    chunks = -(-nb // BLOCKS_PER_CHUNK)
    sizes = [min(BLOCKS_PER_CHUNK, nb - c * BLOCKS_PER_CHUNK) for c in range(chunks)]
    tok = hid.shape[0]
    share = tok // n_mp
    slab = cap * parts
    rows_z = rank // ny
    blocks_a = hid.shape[1] // width

    dp = lax.axis_index("dp")
    mp = lax.axis_index("mp")
    y, z = dp // nz, lax.rem(dp, nz)
    active = lax.rem(dp, n_mp) == mp
    my_k = dp // n_mp

    def mp_peer(d):
        return lax.rem(mp + d, n_mp)

    def y_peer(d):
        return lax.rem(y + d, ny) * nz + z

    def z_of(d):
        return lax.rem(z + d, nz)

    def dp_peer(d):
        return lax.rem(dp + d, n_dp)

    def send(src, dst, ssem, rsem, **device):
        pltpu.make_async_remote_copy(
            src_ref=src, dst_ref=dst, send_sem=ssem, recv_sem=rsem,
            device_id=device, device_id_type=MESH,
        ).start()

    def drain(ref, sem):
        pltpu.make_async_copy(ref, ref, sem).wait()

    def loop(lower, upper, body):
        def step(i, carry):
            body(i)
            return carry
        lax.fori_loop(lower, upper, step, 0)

    barrier = pltpu.get_barrier_semaphore()

    def greet(**device):
        pl.semaphore_signal(barrier, inc=1, device_id=device, device_id_type=MESH)

    loop(1, n_mp, lambda d: greet(mp=mp_peer(d)))
    loop(1, ny, lambda d: greet(dp=y_peer(d)))
    loop(1, nz, lambda d: greet(dp=y * nz + z_of(d)))

    def greet_owner(k):
        owner = k * n_mp + mp

        @pl.when(owner != dp)
        def _():
            greet(dp=owner)

    loop(0, owners, greet_owner)

    @pl.when(active)
    def _():
        loop(1, n_dp, lambda d: greet(dp=dp_peer(d)))
        pltpu.make_async_copy(left_hbm, left_buf, left_sem).start()

    part[:, :rank] = jnp.dot(hid[...], down[...], preferred_element_type=F32)
    part[:, rank:2 * rank] = lax.dot_general(cot[...], up[...], NT, preferred_element_type=F32)

    common = (n_mp - 1) + (ny - 1) + (nz - 1) + owners
    pl.semaphore_wait(barrier, jnp.where(active, common - 1 + n_dp - 1, common))

    def rows(ref, index, count):
        return ref.at[pl.ds(pl.multiple_of(index * count, count), count)]

    loop(1, n_mp, lambda d: send(
        rows(part, mp_peer(d), share), a_recv.at[d - 1], s_a1, r_a1, mp=mp_peer(d)))
    drain(a_recv, r_a1)
    acc = part[pl.ds(pl.multiple_of(mp * share, share), share), :]
    for d in range(n_mp - 1):
        acc = acc + a_recv[d]
    io[mp] = acc.astype(BF16)
    loop(1, n_mp, lambda d: send(io.at[mp], io.at[mp], s_a2, r_a2, mp=mp_peer(d)))
    drain(a_recv.at[pl.ds(0, n_mp - 1)], s_a1)
    drain(io.at[pl.ds(0, n_mp - 1)], r_a2)
    both = io[...].reshape(tok, 2 * rank).astype(F32).T.astype(BF16)
    inner_t, outer_t = both[:rank], both[rank:]

    for c in range(chunks):
        for i in range(sizes[c]):
            b = c * BLOCKS_PER_CHUNK + i
            if b < blocks_a:
                piece = jnp.dot(outer_t, hid[:, b * width:(b + 1) * width], preferred_element_type=F32)
            else:
                at = (b - blocks_a) * width
                piece = jnp.dot(inner_t, cot[:, at:at + width], preferred_element_type=F32)
            gsend[:, :, b * width:(b + 1) * width] = piece.astype(BF16).reshape(ny, rows_z, width)
        span = pl.ds(c * BLOCKS_PER_CHUNK * width, sizes[c] * width)
        loop(1, ny, lambda d: send(
            gsend.at[lax.rem(y + d, ny), :, span], yrecv.at[d - 1, :, span],
            s_y.at[c], r_y.at[c], dp=y_peer(d)))

    scale = ADAPTER_SCALE / (tok * n_dp)
    for c in range(chunks):
        lo, hi = c * BLOCKS_PER_CHUNK * width, (c * BLOCKS_PER_CHUNK + sizes[c]) * width
        drain(yrecv.at[:, :, pl.ds(lo, hi - lo)], r_y.at[c])
        acc = gsend[y, :, lo:hi].astype(F32)
        for d in range(ny - 1):
            acc = acc + yrecv[d, :, lo:hi].astype(F32)
        count = sizes[c] * parts
        for t in range(tile):
            if t < count:
                zstage[c, pl.ds(t, nz, stride=tile), :] = acc[:, t * LANES:(t + 1) * LANES]
            else:
                zstage[c, pl.ds(t, nz, stride=tile), :] = jnp.zeros((nz, LANES), F32)
        zsend[c] = zstage[c].reshape(nz, tile, LANES).astype(BF16)
        loop(1, nz, lambda d: send(
            zsend.at[c, z_of(d)], zrecv.at[c, d - 1], s_z.at[c], r_z.at[c], dp=y * nz + z_of(d)))
    for c in range(chunks):
        drain(zrecv.at[c], r_z.at[c])
        acc = zstage[c, pl.ds(pl.multiple_of(z * tile, tile), tile), :]
        acc = acc + jnp.sum(zrecv[c].astype(F32), axis=0)
        grow[c * tile:(c + 1) * tile] = acc * scale

    keep = mpbuf.shape[1]
    mpbuf[mp] = grow[:keep]
    loop(1, n_mp, lambda d: send(
        grow.at[pl.ds(0, keep)], mpbuf.at[mp], s_d1, r_d1, mp=mp_peer(d)))
    drain(mpbuf.at[pl.ds(0, n_mp - 1)], r_d1)
    slots = n_dp * cap
    for k in range(owners):
        for s in range(cap):
            entry = (k * n_mp + mp) * cap + s
            group, row = tab[entry], tab[slots + entry]
            dsend[k, s * parts:(s + 1) * parts] = mpbuf[group, pl.ds(row, parts), :]

    def to_owner(k):
        owner = k * n_mp + mp

        @pl.when(owner != dp)
        def _():
            send(dsend.at[k], rows(drecv, dp, slab), s_d2, r_d2, dp=owner)

    loop(0, owners, to_owner)

    @pl.when(active)
    def _():
        drecv[pl.ds(pl.multiple_of(dp * slab, slab), slab), :] = dsend[my_k]
        drain(drecv.at[pl.ds(0, (n_dp - 1) * slab)], r_d2)
        pltpu.make_async_copy(left_hbm, left_buf, left_sem).wait()
        for s in range(cap):
            block_t = jnp.concatenate(
                [drecv[pl.ds(s * parts + p, n_dp, stride=slab), :] for p in range(parts)], axis=1)
            result = precondition(block_t, left_buf[s], right_prev[s])
            for p in range(parts):
                fsend[pl.ds(s * parts + p, n_dp, stride=slab), :] = result[:, p * LANES:(p + 1) * LANES]
        loop(1, n_dp, lambda d: send(
            rows(fsend, dp_peer(d), slab), rows(frecv, my_k, slab), s_f1, r_f1, dp=dp_peer(d)))
        frecv[pl.ds(pl.multiple_of(my_k * slab, slab), slab), :] = fsend[
            pl.ds(pl.multiple_of(dp * slab, slab), slab), :]
        drain(frecv.at[pl.ds(0, (owners - 1) * slab)], r_f1)

    @pl.when(jnp.logical_not(active))
    def _():
        drain(frecv, r_f1)

    fb[...] = frecv[...].astype(BF16)
    fmp[mp] = fb[...]
    loop(1, n_mp, lambda d: send(fb, fmp.at[mp], s_f2, r_f2, mp=mp_peer(d)))
    drain(fmp.at[pl.ds(0, n_mp - 1)], r_f2)
    fmpf[...] = fmp[...].astype(F32).reshape(fmpf.shape)
    hrow[...] = jnp.zeros(hrow.shape, F32)
    for b in range(nb):
        row = tab[2 * slots + mp * nb + b]
        hrow[b * parts:(b + 1) * parts] = fmpf[pl.ds(row, parts), :]
    for c in range(chunks):
        fin[c, y, z] = hrow[c * tile:(c + 1) * tile].astype(BF16)
    for c in range(chunks):
        loop(1, nz, lambda d: send(
            fin.at[c, y, z], fin.at[c, y, z], s_fz.at[c], r_fz.at[c], dp=y * nz + z_of(d)))
    for c in range(chunks):
        drain(fin.at[c, 0, pl.ds(0, nz - 1)], r_fz.at[c])
        loop(1, ny, lambda d: send(
            fin.at[c, y], fin.at[c, y], s_fy.at[c], r_fy.at[c], dp=y_peer(d)))
    for c in range(chunks):
        drain(fin.at[c, pl.ds(0, ny - 1)], r_fy.at[c])
        finf[...] = fin[c].astype(F32).reshape(finf.shape)
        for t in range(sizes[c] * parts):
            at = c * tile + t
            piece = finf[pl.ds(t, rank, stride=tile), :]
            if at < blocks_a * parts:
                out_a[at * LANES:(at + 1) * LANES, :] = piece.T.astype(BF16)
            else:
                at -= blocks_a * parts
                out_b[:, at * LANES:(at + 1) * LANES] = piece.astype(BF16)

    drain(io.at[pl.ds(0, n_mp - 1)], s_a2)
    for c in range(chunks):
        lo, hi = c * BLOCKS_PER_CHUNK * width, (c * BLOCKS_PER_CHUNK + sizes[c]) * width
        drain(yrecv.at[:, :, pl.ds(lo, hi - lo)], s_y.at[c])
        drain(zrecv.at[c], s_z.at[c])
        drain(fin.at[c, 0, pl.ds(0, nz - 1)], s_fz.at[c])
        drain(fin.at[c, pl.ds(0, ny - 1)], s_fy.at[c])
    drain(mpbuf.at[pl.ds(0, n_mp - 1)], s_d1)
    drain(fmp.at[pl.ds(0, n_mp - 1)], s_f2)

    @pl.when(active)
    def _():
        drain(dsend.at[pl.ds(0, owners - 1)], s_d2)
        drain(fsend.at[pl.ds(0, (n_dp - 1) * slab)], s_f1)

    @pl.when(jnp.logical_not(active))
    def _():
        drain(dsend, s_d2)


def shards(
    hidden, cotangent, adapter_down, adapter_up, owner_per_block, left_statistics, right_statistics
):
    n_dp, n_mp = lax.axis_size("dp"), lax.axis_size("mp")
    nz = Z_EXTENT
    ny = n_dp // nz
    tok, units = hidden.shape
    features = cotangent.shape[1]
    rank = adapter_down.shape[1]
    nb = owner_per_block.shape[1]
    cap, width = left_statistics.shape[:2]
    parts = width // LANES
    owners = n_dp // n_mp
    tile = BLOCKS_PER_CHUNK * parts
    chunks = -(-nb // BLOCKS_PER_CHUNK)
    slab = cap * parts
    share = tok // n_mp
    keep = -(-nb * parts // 8) * 8

    flat = owner_per_block.reshape(-1)
    count = flat.shape[0]
    order = jnp.arange(count)
    same = (flat[:, None] == flat[None, :]) & (order[None, :] < order[:, None])
    slot = jnp.sum(same.astype(jnp.int32), axis=1)
    hit = (flat * cap + slot)[None, :] == jnp.arange(n_dp * cap)[:, None]
    which = jnp.sum(jnp.where(hit, order[None, :], 0), axis=1).astype(jnp.int32)
    place = lax.rem(flat, n_mp) * (owners * slab) + (flat // n_mp) * slab + slot * parts
    table = jnp.concatenate([which // nb, lax.rem(which, nb) * parts, place]).astype(jnp.int32)

    vmem = pl.BlockSpec(memory_space=pltpu.VMEM)
    dma = pltpu.SemaphoreType.DMA
    cfg = (n_dp, n_mp, ny, nz, rank, width, nb)
    return pl.pallas_call(
        functools.partial(kernel, cfg),
        out_shape=(
            jax.ShapeDtypeStruct((units, rank), BF16),
            jax.ShapeDtypeStruct((rank, features), BF16),
        ),
        in_specs=[pl.BlockSpec(memory_space=pltpu.SMEM)] + [vmem] * 4
        + [pl.BlockSpec(memory_space=pl.ANY), vmem],
        out_specs=(vmem, vmem),
        scratch_shapes=[
            pltpu.VMEM((tok, 2 * rank), F32),
            pltpu.VMEM((n_mp - 1, share, 2 * rank), F32),
            pltpu.VMEM((n_mp, share, 2 * rank), BF16),
            pltpu.VMEM((ny, rank // ny, nb * width), BF16),
            pltpu.VMEM((ny - 1, rank // ny, nb * width), BF16),
            pltpu.VMEM((chunks, nz * tile, LANES), F32),
            pltpu.VMEM((chunks, nz, tile, LANES), BF16),
            pltpu.VMEM((chunks, nz - 1, tile, LANES), BF16),
            pltpu.VMEM((chunks * tile, LANES), F32),
            pltpu.VMEM((n_mp, keep, LANES), F32),
            pltpu.VMEM((owners, slab, LANES), F32),
            pltpu.VMEM((n_dp * slab, LANES), F32),
            pltpu.VMEM((cap, width, width), F32),
            pltpu.VMEM((n_dp * slab, LANES), F32),
            pltpu.VMEM((owners * slab, LANES), F32),
            pltpu.VMEM((owners * slab, LANES), BF16),
            pltpu.VMEM((n_mp, owners * slab, LANES), BF16),
            pltpu.VMEM((n_mp * owners * slab, LANES), F32),
            pltpu.VMEM((chunks * tile, LANES), F32),
            pltpu.VMEM((chunks, ny, nz, tile, LANES), BF16),
            pltpu.VMEM((rank * tile, LANES), F32),
            dma, dma, dma, dma, dma,
            dma((chunks,)), dma((chunks,)), dma((chunks,)), dma((chunks,)),
            dma, dma, dma, dma, dma, dma, dma, dma,
            dma((chunks,)), dma((chunks,)), dma((chunks,)), dma((chunks,)),
        ],
        compiler_params=pltpu.CompilerParams(
            collective_id=0, has_side_effects=True, vmem_limit_bytes=48 * 1024 * 1024
        ),
    )(table, hidden, cotangent, adapter_down, adapter_up, left_statistics, right_statistics)


def solution(mesh):
    return jax.shard_map(
        shards,
        mesh=mesh,
        in_specs=(
            P("dp", "mp"),
            P("dp", "mp"),
            P("mp", None),
            P(None, "mp"),
            P(),
            P("dp", None, None),
            P("dp", None, None),
        ),
        out_specs=(P("mp", None), P(None, "mp")),
        check_vma=False,
    )
```

```python
import functools

import jax
import jax.numpy as jnp
from jax import lax
from jax.experimental import pallas as pl
from jax.experimental.pallas import tpu as pltpu
from jax.sharding import PartitionSpec as P

Z_EXTENT = 16
BLOCKS_PER_CHUNK = 4
LANES = 128

ADAPTER_SCALE = 2.0
BETA_STAT = 0.9
EPS_NORM = 1e-06
MESH = pl.DeviceIdType.MESH
BF16 = jnp.bfloat16
F32 = jnp.float32

NN = (((1,), (0,)), ((), ()))
NT = (((1,), (1,)), ((), ()))
TN = (((0,), (0,)), ((), ()))


def split(value):
    high = value.astype(BF16)
    return high, (value - high.astype(F32)).astype(BF16)


def dot3(first, second, dims):
    (fh, fl), (sh, sl) = split(first), split(second)
    return dot1(fh, sh, dims) + (dot1(fl, sh, dims) + dot1(fh, sl, dims))


def dot1(first, second, dims):
    return lax.dot_general(
        first.astype(BF16), second.astype(BF16), dims, preferred_element_type=F32)


def eye(n):
    return (
        lax.broadcasted_iota(jnp.int32, (n, n), 0) == lax.broadcasted_iota(jnp.int32, (n, n), 1)
    ).astype(F32)


def total(value):
    return jnp.sum(jnp.sum(value, axis=0, keepdims=True), axis=1, keepdims=True)


def precondition(blocks, lefts, rights):
    rank, width = blocks[0].shape
    n = range(len(blocks))
    lefts = [BETA_STAT * lefts[i] + (1.0 - BETA_STAT) * dot1(blocks[i], blocks[i], TN) for i in n]
    rights = [BETA_STAT * rights[i] + (1.0 - BETA_STAT) * dot1(blocks[i], blocks[i], NT) for i in n]
    short = [v.astype(BF16) for v in lefts]
    left_z = [5.0 / (2.0 * jnp.sqrt(total(v * v))) for v in lefts]
    right_z = [5.0 / (2.0 * jnp.sqrt(total(v * v))) for v in rights]
    right_m = [right_z[i] * rights[i] for i in n]

    moved = [dot1(blocks[i], short[i], NN) * left_z[i] for i in n]
    small = right_m
    for _ in range(4):
        moved = [(5.0 * moved[i] - dot1(moved[i], short[i], NN) * left_z[i]) / 4.0 for i in n]
        small = [(5.0 * small[i] - dot1(right_m[i], small[i], NN)) / 4.0 for i in n]
    outs = [(5.0 * blocks[i] - moved[i]) / 4.0 for i in n]
    roots = [(5.0 * eye(rank) - small[i]) / 4.0 for i in n]
    outs = [(5.0 * outs[i] - dot1(outs[i], short[i], NN) * left_z[i]) / 4.0 for i in n]
    roots = [(5.0 * roots[i] - dot1(right_m[i], roots[i], NN)) / 4.0 for i in n]
    gains = [jnp.sqrt(jnp.sqrt(left_z[i])) * jnp.sqrt(jnp.sqrt(right_z[i])) for i in n]
    outs = [dot3(roots[i], outs[i], NN) * gains[i] for i in n]
    return [v * lax.rsqrt(total(v * v) / (rank * width) + EPS_NORM) for v in outs]


def kernel(
    cfg,
    owner_ref, hid_hbm, cot_hbm, down_hbm, up_hbm, left_hbm, right_hbm,
    out_a, out_b,
    hid, cot, down, up, right_prev, left_buf, pbuf, gsend, yrecv, zstage, zsend, zrecv,
    rstage, rsend, rrecv, grow, mpbuf, dsend, drecv, fsend, frecv, fb, fmp, fmpf, hrow,
    fin, finr, finf, finrf, ystage,
    in_sem, left_sem, s_a, r_a, s_y, r_y, s_z, r_z, s_d1, r_d1, s_d2, r_d2,
    s_f1, r_f1, s_f2, r_f2, s_fz, r_fz, s_fy, r_fy, own_sem,
):
    n_dp, n_mp, ny, nz, rank, width, nb, cap = cfg
    parts = width // LANES
    owners = n_dp // n_mp
    tile = BLOCKS_PER_CHUNK * parts
    whole = nb // BLOCKS_PER_CHUNK
    chunks = whole + 1
    rest = (nb - whole * BLOCKS_PER_CHUNK) * parts
    sizes = [tile] * whole + [rest]
    tok, units = hid.shape
    slab = cap * parts
    rows_y = rank // ny
    blocks_a = units // width

    dp = lax.axis_index("dp")
    mp = lax.axis_index("mp")
    y, z = dp // nz, lax.rem(dp, nz)
    active = lax.rem(dp, n_mp) == mp
    my_k = dp // n_mp

    def mp_peer(d):
        return lax.rem(mp + d, n_mp)

    def y_of(d):
        return lax.rem(y + d, ny)

    def z_of(d):
        return lax.rem(z + d, nz)

    def far_first(d):
        half = nz // 2
        step = d // 2
        return jnp.where(lax.rem(d, 2) == 0, half + step, half - step)

    def send(src, dst, ssem, rsem, **device):
        pltpu.make_async_remote_copy(
            src_ref=src, dst_ref=dst, send_sem=ssem, recv_sem=rsem,
            device_id=device, device_id_type=MESH,
        ).start()

    def drain(ref, sem):
        pltpu.make_async_copy(ref, ref, sem).wait()

    def loop(lower, upper, body):
        def step(i, carry):
            body(i)
            return carry
        lax.fori_loop(lower, upper, step, 0)

    def rows(index, count):
        return pl.ds(pl.multiple_of(index * count, count), count)

    cuts = 4 if units % (4 * LANES) == 0 else 1
    span_in = units // cuts
    loads = []
    for i in range(cuts):
        at = pl.ds(i * span_in, span_in)
        loads.append(pltpu.make_async_copy(hid_hbm.at[:, at], hid.at[:, at], in_sem.at[2 * i]))
        loads.append(pltpu.make_async_copy(down_hbm.at[:, at], down.at[:, at], in_sem.at[2 * i + 1]))
    loads.append(pltpu.make_async_copy(cot_hbm, cot, in_sem.at[2 * cuts]))
    loads.append(pltpu.make_async_copy(up_hbm, up, in_sem.at[2 * cuts + 1]))
    for copy in loads:
        copy.start()
    late = [
        pltpu.make_async_copy(left_hbm, left_buf, left_sem.at[0]),
        pltpu.make_async_copy(right_hbm, right_prev, left_sem.at[1]),
    ]

    barrier = pltpu.get_barrier_semaphore()

    def greet(**device):
        pl.semaphore_signal(barrier, inc=1, device_id=device, device_id_type=MESH)

    loop(1, nz, lambda d: greet(dp=y * nz + z_of(far_first(d))))
    loop(1, n_mp, lambda d: greet(mp=mp_peer(d)))
    loop(1, ny, lambda d: greet(dp=y_of(d) * nz + z))

    def greet_owner(k):
        owner = k * n_mp + mp

        @pl.when(owner != dp)
        def _():
            greet(dp=owner)

    loop(0, owners, greet_owner)

    @pl.when(active)
    def _():
        loop(1, n_dp, lambda d: greet(dp=lax.rem(dp + d, n_dp)))

    acc = jnp.zeros((rank, tok), F32)
    for i in range(cuts):
        loads[2 * i].wait()
        loads[2 * i + 1].wait()
        at = pl.ds(i * span_in, span_in)
        acc = acc + dot1(down[:, at], hid[:, at], NT)
    pbuf[mp, :rank] = acc.astype(BF16)
    loads[-2].wait()
    loads[-1].wait()
    pbuf[mp, rank:] = dot1(up[...], cot[...], NT).astype(BF16)

    common = (n_mp - 1) + (ny - 1) + (nz - 1) + owners
    pl.semaphore_wait(barrier, jnp.where(active, common - 1 + n_dp - 1, common))

    loop(1, n_mp, lambda d: send(pbuf.at[mp], pbuf.at[mp], s_a, r_a, mp=mp_peer(d)))

    @pl.when(active)
    def _():
        for copy in late:
            copy.start()

    drain(pbuf.at[pl.ds(0, n_mp - 1)], r_a)
    acc = pbuf[0].astype(F32)
    for d in range(1, n_mp):
        acc = acc + pbuf[d].astype(F32)
    inner_t, outer_t = acc[:rank].astype(BF16), acc[rank:].astype(BF16)

    def lanes(c):
        return c * tile * LANES, c * tile * LANES + sizes[c] * LANES

    for c in range(chunks):
        lo, hi = lanes(c)
        for at in range(lo, hi, width):
            if at < units:
                piece = dot1(outer_t, hid[:, at:at + width], NN)
            else:
                piece = dot1(inner_t, cot[:, at - units:at - units + width], NN)
            gsend[:, :, at:at + width] = piece.astype(BF16).reshape(ny, rows_y, width)
        span = pl.ds(lo, hi - lo)
        loop(1, ny, lambda d: send(
            gsend.at[y_of(d), :, span], yrecv.at[d - 1, :, span],
            s_y.at[c], r_y.at[c], dp=y_of(d) * nz + z))

    groups = n_mp
    mine = [owner_ref[mp, b] for b in range(nb)]
    zero = jnp.int32(0)

    def scan(i, carry):
        first, second, slot = carry
        g = groups * nb - 1 - i
        value = owner_ref[g // nb, lax.rem(g, nb)]
        hits = [value == k * n_mp + mp for k in range(owners)]
        second = tuple(jnp.where(h, f, s) for h, f, s in zip(hits, first, second))
        first = tuple(jnp.where(h, g, f) for h, f in zip(hits, first))
        slot = tuple(
            v + jnp.where(value == mine[b], jnp.where(g < mp * nb + b, 1, 0), 0)
            for b, v in enumerate(slot))
        return first, second, slot

    first, second, slot = lax.fori_loop(
        0, groups * nb, scan, ((zero,) * owners, (zero,) * owners, (zero,) * nb))
    places = [
        lax.rem(mine[b], n_mp) * (owners * slab) + (mine[b] // n_mp) * slab + slot[b] * parts
        for b in range(nb)]

    scale = ADAPTER_SCALE / (tok * n_dp)
    for c in range(chunks):
        lo, hi = lanes(c)
        drain(yrecv.at[:, :, pl.ds(lo, hi - lo)], r_y.at[c])
        acc = gsend[y, :, lo:hi].astype(F32)
        for d in range(ny - 1):
            acc = acc + yrecv[d, :, lo:hi].astype(F32)
        if c < whole:
            for t in range(tile):
                zstage[c, pl.ds(t, nz, stride=tile), :] = acc[:, t * LANES:(t + 1) * LANES]
            zsend[c] = zstage[c].reshape(nz, tile, LANES).astype(BF16)
            src, dst = zsend.at[c], zrecv.at[c]
        else:
            for t in range(rest):
                rstage[pl.ds(t, nz, stride=8), :] = acc[:, t * LANES:(t + 1) * LANES]
            for i in range(nz):
                rsend[i] = rstage[8 * i:8 * i + rest, :]
            src, dst = rsend, rrecv

        def scatter(i):
            d = far_first(i)
            send(src.at[z_of(d)], dst.at[d - 1], s_z.at[c], r_z.at[c], dp=y * nz + z_of(d))

        loop(1, nz, scatter)
    for c in range(chunks):
        if c < whole:
            drain(zrecv.at[c], r_z.at[c])
            acc = zstage[c, rows(z, tile), :] + jnp.sum(zrecv[c].astype(F32), axis=0)
            grow[c * tile:(c + 1) * tile] = acc * scale
        else:
            drain(rrecv, r_z.at[c])
            acc = rsend[z] + jnp.sum(rrecv[...], axis=0)
            grow[c * tile:c * tile + rest] = acc * scale
            if grow.shape[0] > c * tile + rest:
                grow[c * tile + rest:] = jnp.zeros((grow.shape[0] - c * tile - rest, LANES), F32)

    mpbuf[mp] = grow[...]
    loop(1, n_mp, lambda d: send(grow, mpbuf.at[mp], s_d1, r_d1, mp=mp_peer(d)))
    drain(mpbuf.at[pl.ds(0, n_mp - 1)], r_d1)
    for k in range(owners):
        for s, g in enumerate((first[k], second[k])):
            dsend[k, s * parts:(s + 1) * parts] = mpbuf[
                g // nb, pl.ds(lax.rem(g, nb) * parts, parts), :]

    def to_owner(k):
        owner = k * n_mp + mp

        @pl.when(owner != dp)
        def _():
            send(dsend.at[k], drecv.at[rows(dp, slab)], s_d2, r_d2, dp=owner)

    loop(0, owners, to_owner)

    @pl.when(active)
    def _():
        drecv[rows(dp, slab), :] = dsend[my_k]
        for copy in late:
            copy.wait()
        drain(drecv.at[pl.ds(0, (n_dp - 1) * slab)], r_d2)
        blocks = [
            jnp.concatenate(
                [drecv[pl.ds(s * parts + p, n_dp, stride=slab), :] for p in range(parts)], axis=1)
            for s in range(cap)]
        results = precondition(
            blocks, [left_buf[s] for s in range(cap)], [right_prev[s] for s in range(cap)])
        for s in range(cap):
            for p in range(parts):
                fsend[pl.ds(s * parts + p, n_dp, stride=slab), :] = results[s][
                    :, p * LANES:(p + 1) * LANES]

        def to_home(i):
            d = i // ny + 1
            home = y_of(lax.rem(i, ny)) * nz + z_of(far_first(d))
            send(fsend.at[rows(home, slab)], frecv.at[rows(my_k, slab)], s_f1, r_f1, dp=home)

        loop(0, (nz - 1) * ny, to_home)

        def to_column(d):
            home = y_of(d) * nz + z
            send(fsend.at[rows(home, slab)], frecv.at[rows(my_k, slab)], s_f1, r_f1, dp=home)

        loop(1, ny, to_column)
        frecv[rows(my_k, slab), :] = fsend[rows(dp, slab), :]
        drain(frecv.at[pl.ds(0, (owners - 1) * slab)], r_f1)

    @pl.when(jnp.logical_not(active))
    def _():
        drain(frecv, r_f1)

    fb[...] = frecv[...].astype(BF16)
    fmp[mp] = fb[...]
    loop(1, n_mp, lambda d: send(fb, fmp.at[mp], s_f2, r_f2, mp=mp_peer(d)))
    drain(fmp.at[pl.ds(0, n_mp - 1)], r_f2)
    fmpf[...] = fmp[...].astype(F32).reshape(fmpf.shape)
    for b in range(nb):
        hrow[b * parts:(b + 1) * parts] = fmpf[pl.ds(places[b], parts), :]
    for c in range(chunks):
        if c < whole:
            fin[c, z] = hrow[c * tile:(c + 1) * tile].astype(BF16)
            buf = fin.at[c]
        else:
            finr[z] = hrow[c * tile:c * tile + rest]
            buf = finr

        def spread(i):
            d = far_first(i)
            send(buf.at[z], buf.at[z], s_fz.at[c], r_fz.at[c], dp=y * nz + z_of(d))

        loop(1, nz, spread)

    def spans(c):
        lo, hi = lanes(c)
        found = []
        if lo < units:
            found.append((out_a, lo, lo, min(hi, units) - lo))
        if hi > units:
            start = max(lo, units)
            found.append((out_b, start, start - units, hi - start))
        return found

    mine_rows = rows(y, rows_y)
    for c in range(chunks):
        if c < whole:
            drain(fin.at[c, pl.ds(0, nz - 1)], r_fz.at[c])
            finf[...] = fin[c].astype(F32).reshape(finf.shape)
            for t in range(tile):
                at = (c * tile + t) * LANES
                ystage[:, at:at + LANES] = finf[pl.ds(t, nz, stride=tile), :].astype(BF16)
        else:
            drain(finr.at[pl.ds(0, nz - 1)], r_fz.at[c])
            for i in range(nz):
                finrf[8 * i:8 * i + rest, :] = finr[i]
            for t in range(rest):
                at = (c * tile + t) * LANES
                ystage[:, at:at + LANES] = finrf[pl.ds(t, nz, stride=8), :].astype(BF16)
        for j, (out, src, dst, count) in enumerate(spans(c)):
            loop(1, ny, lambda d: send(
                ystage.at[:, pl.ds(src, count)], out.at[mine_rows, pl.ds(dst, count)],
                s_fy.at[2 * c + j], r_fy.at[2 * c + j], dp=y_of(d) * nz + z))
            pltpu.make_async_copy(
                ystage.at[:, pl.ds(src, count)], out.at[mine_rows, pl.ds(dst, count)],
                own_sem.at[2 * c + j]).start()
    for c in range(chunks):
        for j, (out, src, dst, count) in enumerate(spans(c)):
            arrived = out.at[pl.ds(0, rank - rows_y), pl.ds(dst, count)]
            drain(arrived, r_fy.at[2 * c + j])
            drain(arrived, s_fy.at[2 * c + j])
            pltpu.make_async_copy(
                ystage.at[:, pl.ds(src, count)], out.at[mine_rows, pl.ds(dst, count)],
                own_sem.at[2 * c + j]).wait()

    drain(pbuf.at[pl.ds(0, n_mp - 1)], s_a)
    for c in range(chunks):
        lo, hi = lanes(c)
        drain(yrecv.at[:, :, pl.ds(lo, hi - lo)], s_y.at[c])
        if c < whole:
            drain(zrecv.at[c], s_z.at[c])
            drain(fin.at[c, pl.ds(0, nz - 1)], s_fz.at[c])
        else:
            drain(rrecv, s_z.at[c])
            drain(finr.at[pl.ds(0, nz - 1)], s_fz.at[c])
    drain(mpbuf.at[pl.ds(0, n_mp - 1)], s_d1)
    drain(fmp.at[pl.ds(0, n_mp - 1)], s_f2)

    @pl.when(active)
    def _():
        drain(dsend.at[pl.ds(0, owners - 1)], s_d2)
        drain(fsend.at[pl.ds(0, (n_dp - 1) * slab)], s_f1)

    @pl.when(jnp.logical_not(active))
    def _():
        drain(dsend, s_d2)


def placing(first_in, second_in, first_out, second_out):
    first_out[...] = first_in[...]
    second_out[...] = second_in[...]


def shards(
    hidden, cotangent, adapter_down, adapter_up, owner_per_block, left_statistics, right_statistics
):
    n_dp, n_mp = lax.axis_size("dp"), lax.axis_size("mp")
    nz = Z_EXTENT
    ny = n_dp // nz
    tok, units = hidden.shape
    features = cotangent.shape[1]
    rank = adapter_down.shape[1]
    nb = owner_per_block.shape[1]
    cap, width = left_statistics.shape[:2]
    parts = width // LANES
    owners = n_dp // n_mp
    tile = BLOCKS_PER_CHUNK * parts
    whole = nb // BLOCKS_PER_CHUNK
    chunks = whole + 1
    rest = (nb - whole * BLOCKS_PER_CHUNK) * parts
    slab = cap * parts
    keep = -(-nb * parts // 8) * 8
    rows_y = rank // ny

    any_space = pl.BlockSpec(memory_space=pl.ANY)
    dma = pltpu.SemaphoreType.DMA
    vmem = pltpu.VMEM
    cfg = (n_dp, n_mp, ny, nz, rank, width, nb, cap)
    shapes = (
        jax.ShapeDtypeStruct((rank, units), BF16),
        jax.ShapeDtypeStruct((rank, features), BF16),
    )
    update_a, update_b = pl.pallas_call(
        functools.partial(kernel, cfg),
        out_shape=shapes,
        in_specs=[pl.BlockSpec(memory_space=pltpu.SMEM)] + [any_space] * 6,
        out_specs=(any_space, any_space),
        scratch_shapes=[
            vmem((tok, units), BF16),
            vmem((tok, features), BF16),
            vmem((rank, units), BF16),
            vmem((rank, features), BF16),
            vmem((cap, rank, rank), F32),
            vmem((cap, width, width), F32),
            vmem((n_mp, 2 * rank, tok), BF16),
            vmem((ny, rows_y, nb * width), BF16),
            vmem((ny - 1, rows_y, nb * width), BF16),
            vmem((whole, nz * tile, LANES), F32),
            vmem((whole, nz, tile, LANES), BF16),
            vmem((whole, nz - 1, tile, LANES), BF16),
            vmem((nz * 8, LANES), F32),
            vmem((nz, rest, LANES), F32),
            vmem((nz - 1, rest, LANES), F32),
            vmem((keep, LANES), F32),
            vmem((n_mp, keep, LANES), F32),
            vmem((owners, slab, LANES), F32),
            vmem((n_dp * slab, LANES), F32),
            vmem((n_dp * slab, LANES), F32),
            vmem((owners * slab, LANES), F32),
            vmem((owners * slab, LANES), BF16),
            vmem((n_mp, owners * slab, LANES), BF16),
            vmem((n_mp * owners * slab, LANES), F32),
            vmem((keep, LANES), F32),
            vmem((whole, nz, tile, LANES), BF16),
            vmem((nz, rest, LANES), F32),
            vmem((nz * tile, LANES), F32),
            vmem((nz * 8, LANES), F32),
            vmem((rows_y, nb * width), BF16),
            dma((10,)), dma((2,)), dma, dma,
            dma((chunks,)), dma((chunks,)), dma((chunks,)), dma((chunks,)),
            dma, dma, dma, dma, dma, dma, dma, dma,
            dma((chunks,)), dma((chunks,)),
            dma((2 * chunks,)), dma((2 * chunks,)), dma((2 * chunks,)),
        ],
        compiler_params=pltpu.CompilerParams(
            collective_id=0, has_side_effects=True, vmem_limit_bytes=58 * 1024 * 1024
        ),
    )(
        owner_per_block, hidden, cotangent, adapter_down.T, adapter_up,
        left_statistics, right_statistics,
    )
    update_a, update_b = pl.pallas_call(
        placing,
        out_shape=shapes,
        in_specs=[pl.BlockSpec(memory_space=vmem)] * 2,
        out_specs=(pl.BlockSpec(memory_space=vmem), pl.BlockSpec(memory_space=vmem)),
        compiler_params=pltpu.CompilerParams(vmem_limit_bytes=58 * 1024 * 1024),
    )(update_a, update_b)
    return update_a.T, update_b


def solution(mesh):
    return jax.shard_map(
        shards,
        mesh=mesh,
        in_specs=(
            P("dp", "mp"),
            P("dp", "mp"),
            P("mp", None),
            P(None, "mp"),
            P(),
            P("dp", None, None),
            P("dp", None, None),
        ),
        out_specs=(P("mp", None), P(None, "mp")),
        check_vma=False,
    )
```

```python
import functools

import jax
import jax.numpy as jnp
from jax import lax
from jax.experimental import pallas as pl
from jax.experimental.pallas import tpu as pltpu
from jax.sharding import PartitionSpec as P

Z_EXTENT = 16
BLOCKS_PER_CHUNK = 4
LANES = 128

ADAPTER_SCALE = 2.0
BETA_STAT = 0.9
EPS_NORM = 1e-06
MESH = pl.DeviceIdType.MESH
BF16 = jnp.bfloat16
F32 = jnp.float32

NN = (((1,), (0,)), ((), ()))
NT = (((1,), (1,)), ((), ()))
TN = (((0,), (0,)), ((), ()))


def split(value):
    high = value.astype(BF16)
    return high, (value - high.astype(F32)).astype(BF16)


def dot3(first, second, dims):
    (fh, fl), (sh, sl) = split(first), split(second)
    return dot1(fh, sh, dims) + (dot1(fl, sh, dims) + dot1(fh, sl, dims))


def dot1(first, second, dims):
    return lax.dot_general(
        first.astype(BF16), second.astype(BF16), dims, preferred_element_type=F32)


def eye(n):
    return (
        lax.broadcasted_iota(jnp.int32, (n, n), 0) == lax.broadcasted_iota(jnp.int32, (n, n), 1)
    ).astype(F32)


def total(value):
    return jnp.sum(jnp.sum(value, axis=0, keepdims=True), axis=1, keepdims=True)


def precondition(blocks, lefts, rights):
    rank, width = blocks[0].shape
    n = range(len(blocks))
    lefts = [BETA_STAT * lefts[i] + (1.0 - BETA_STAT) * dot1(blocks[i], blocks[i], TN) for i in n]
    rights = [BETA_STAT * rights[i] + (1.0 - BETA_STAT) * dot1(blocks[i], blocks[i], NT) for i in n]
    short = [v.astype(BF16) for v in lefts]
    left_z = [5.0 / (2.0 * jnp.sqrt(total(v * v))) for v in lefts]
    right_z = [5.0 / (2.0 * jnp.sqrt(total(v * v))) for v in rights]
    right_m = [right_z[i] * rights[i] for i in n]

    moved = [dot1(blocks[i], short[i], NN) * left_z[i] for i in n]
    small = right_m
    for _ in range(4):
        moved = [(5.0 * moved[i] - dot1(moved[i], short[i], NN) * left_z[i]) / 4.0 for i in n]
        small = [(5.0 * small[i] - dot1(right_m[i], small[i], NN)) / 4.0 for i in n]
    outs = [(5.0 * blocks[i] - moved[i]) / 4.0 for i in n]
    roots = [(5.0 * eye(rank) - small[i]) / 4.0 for i in n]
    outs = [(5.0 * outs[i] - dot1(outs[i], short[i], NN) * left_z[i]) / 4.0 for i in n]
    roots = [(5.0 * roots[i] - dot1(right_m[i], roots[i], NN)) / 4.0 for i in n]
    gains = [jnp.sqrt(jnp.sqrt(left_z[i])) * jnp.sqrt(jnp.sqrt(right_z[i])) for i in n]
    outs = [dot3(roots[i], outs[i], NN) * gains[i] for i in n]
    return [v * lax.rsqrt(total(v * v) / (rank * width) + EPS_NORM) for v in outs]


def kernel(
    cfg,
    owner_ref, hid_hbm, cot_hbm, down_hbm, up_hbm, left_hbm, right_hbm,
    out_a, out_b,
    hid, cot, down, up, right_prev, left_buf, pbuf, gsend, yrecv, zstage, zsend, zrecv,
    rstage, rsend, rrecv, grow, mpbuf, dsend, drecv, fsend, frecv, fb, fmp, fmpf, hrow,
    fin, finr, finf, finrf, ystage,
    in_sem, left_sem, s_a, r_a, s_y, r_y, s_z, r_z, s_d1, r_d1, s_d2, r_d2,
    s_f1, r_f1, s_f2, r_f2, s_fz, r_fz, s_fy, r_fy, own_sem,
):
    n_dp, n_mp, ny, nz, rank, width, nb, cap = cfg
    parts = width // LANES
    owners = n_dp // n_mp
    tile = BLOCKS_PER_CHUNK * parts
    whole = nb // BLOCKS_PER_CHUNK
    chunks = whole + 1
    rest = (nb - whole * BLOCKS_PER_CHUNK) * parts
    sizes = [tile] * whole + [rest]
    tok, units = hid.shape
    slab = cap * parts
    half = nz // 2
    pair = 2 * slab
    rows_y = rank // ny
    blocks_a = units // width

    dp = lax.axis_index("dp")
    mp = lax.axis_index("mp")
    y, z = dp // nz, lax.rem(dp, nz)
    active = lax.rem(dp, n_mp) == mp
    my_k = dp // n_mp

    def mp_peer(d):
        return lax.rem(mp + d, n_mp)

    def y_of(d):
        return lax.rem(y + d, ny)

    def z_of(d):
        return lax.rem(z + d, nz)

    def far_first(d):
        step = d // 2
        return jnp.where(lax.rem(d, 2) == 0, half + step, half - step)

    def send(src, dst, ssem, rsem, **device):
        pltpu.make_async_remote_copy(
            src_ref=src, dst_ref=dst, send_sem=ssem, recv_sem=rsem,
            device_id=device, device_id_type=MESH,
        ).start()

    def drain(ref, sem):
        pltpu.make_async_copy(ref, ref, sem).wait()

    def loop(lower, upper, body):
        def step(i, carry):
            body(i)
            return carry
        lax.fori_loop(lower, upper, step, 0)

    def rows(index, count):
        return pl.ds(pl.multiple_of(index * count, count), count)

    cuts = 4 if units % (4 * LANES) == 0 else 1
    span_in = units // cuts
    loads = []
    for i in range(cuts):
        at = pl.ds(i * span_in, span_in)
        loads.append(pltpu.make_async_copy(hid_hbm.at[:, at], hid.at[:, at], in_sem.at[2 * i]))
        loads.append(pltpu.make_async_copy(down_hbm.at[:, at], down.at[:, at], in_sem.at[2 * i + 1]))
    loads.append(pltpu.make_async_copy(cot_hbm, cot, in_sem.at[2 * cuts]))
    loads.append(pltpu.make_async_copy(up_hbm, up, in_sem.at[2 * cuts + 1]))
    for copy in loads:
        copy.start()
    late = [
        pltpu.make_async_copy(left_hbm, left_buf, left_sem.at[0]),
        pltpu.make_async_copy(right_hbm, right_prev, left_sem.at[1]),
    ]

    barrier = pltpu.get_barrier_semaphore()

    def greet(**device):
        pl.semaphore_signal(barrier, inc=1, device_id=device, device_id_type=MESH)

    loop(1, nz, lambda d: greet(dp=y * nz + z_of(far_first(d))))
    loop(1, n_mp, lambda d: greet(mp=mp_peer(d)))
    loop(1, ny, lambda d: greet(dp=y_of(d) * nz + z))

    acc = jnp.zeros((rank, tok), F32)
    for i in range(cuts):
        loads[2 * i].wait()
        loads[2 * i + 1].wait()
        at = pl.ds(i * span_in, span_in)
        acc = acc + dot1(down[:, at], hid[:, at], NT)
    pbuf[mp, :rank] = acc.astype(BF16)
    loads[-2].wait()
    loads[-1].wait()
    pbuf[mp, rank:] = dot1(up[...], cot[...], NT).astype(BF16)

    pl.semaphore_wait(barrier, (n_mp - 1) + (ny - 1) + (nz - 1))

    loop(1, n_mp, lambda d: send(pbuf.at[mp], pbuf.at[mp], s_a, r_a, mp=mp_peer(d)))

    @pl.when(active)
    def _():
        for copy in late:
            copy.start()

    drain(pbuf.at[pl.ds(0, n_mp - 1)], r_a)
    acc = pbuf[0].astype(F32)
    for d in range(1, n_mp):
        acc = acc + pbuf[d].astype(F32)
    inner_t, outer_t = acc[:rank].astype(BF16), acc[rank:].astype(BF16)

    def lanes(c):
        return c * tile * LANES, c * tile * LANES + sizes[c] * LANES

    for c in range(chunks):
        lo, hi = lanes(c)
        for at in range(lo, hi, width):
            if at < units:
                piece = dot1(outer_t, hid[:, at:at + width], NN)
            else:
                piece = dot1(inner_t, cot[:, at - units:at - units + width], NN)
            gsend[:, :, at:at + width] = piece.astype(BF16).reshape(ny, rows_y, width)
        span = pl.ds(lo, hi - lo)
        loop(1, ny, lambda d: send(
            gsend.at[y_of(d), :, span], yrecv.at[d - 1, :, span],
            s_y.at[c], r_y.at[c], dp=y_of(d) * nz + z))

    groups = n_mp
    mine = [owner_ref[mp, b] for b in range(nb)]
    zero = jnp.int32(0)

    def scan(i, carry):
        first, second, slot = carry
        g = groups * nb - 1 - i
        value = owner_ref[g // nb, lax.rem(g, nb)]
        hits = [value == k * n_mp + mp for k in range(owners)]
        second = tuple(jnp.where(h, f, s) for h, f, s in zip(hits, first, second))
        first = tuple(jnp.where(h, g, f) for h, f in zip(hits, first))
        slot = tuple(
            v + jnp.where(value == mine[b], jnp.where(g < mp * nb + b, 1, 0), 0)
            for b, v in enumerate(slot))
        return first, second, slot

    first, second, slot = lax.fori_loop(
        0, groups * nb, scan, ((zero,) * owners, (zero,) * owners, (zero,) * nb))
    places = [
        lax.rem(mine[b], n_mp) * (owners * pair) + (mine[b] // n_mp) * pair + slot[b] * parts
        for b in range(nb)]

    scale = ADAPTER_SCALE / (tok * n_dp)
    for c in range(chunks):
        lo, hi = lanes(c)
        drain(yrecv.at[:, :, pl.ds(lo, hi - lo)], r_y.at[c])
        acc = gsend[y, :, lo:hi].astype(F32)
        for d in range(ny - 1):
            acc = acc + yrecv[d, :, lo:hi].astype(F32)
        if c < whole:
            for t in range(tile):
                zstage[c, pl.ds(t, nz, stride=tile), :] = acc[:, t * LANES:(t + 1) * LANES]
            zsend[c] = zstage[c].reshape(nz, tile, LANES).astype(BF16)
            src, dst = zsend.at[c], zrecv.at[c]
        else:
            for t in range(rest):
                rstage[pl.ds(t, nz, stride=8), :] = acc[:, t * LANES:(t + 1) * LANES]
            for i in range(nz):
                rsend[i] = rstage[8 * i:8 * i + rest, :]
            src, dst = rsend, rrecv

        def scatter(i):
            d = far_first(i)
            send(src.at[z_of(d)], dst.at[d - 1], s_z.at[c], r_z.at[c], dp=y * nz + z_of(d))

        loop(1, nz, scatter)
    for c in range(chunks):
        if c < whole:
            drain(zrecv.at[c], r_z.at[c])
            acc = zstage[c, rows(z, tile), :] + jnp.sum(zrecv[c].astype(F32), axis=0)
            grow[c * tile:(c + 1) * tile] = acc * scale
        else:
            drain(rrecv, r_z.at[c])
            acc = rsend[z] + jnp.sum(rrecv[...], axis=0)
            grow[c * tile:c * tile + rest] = acc * scale
            if grow.shape[0] > c * tile + rest:
                grow[c * tile + rest:] = jnp.zeros((grow.shape[0] - c * tile - rest, LANES), F32)

    mpbuf[mp] = grow[...]
    loop(1, n_mp, lambda d: send(grow, mpbuf.at[mp], s_d1, r_d1, mp=mp_peer(d)))
    drain(mpbuf.at[pl.ds(0, n_mp - 1)], r_d1)
    for k in range(owners):
        for s, g in enumerate((first[k], second[k])):
            dsend[k, s * parts:(s + 1) * parts] = mpbuf[
                g // nb, pl.ds(lax.rem(g, nb) * parts, parts), :]

    def to_owner(k):
        owner = k * n_mp + mp

        @pl.when(owner != dp)
        def _():
            send(dsend.at[k], drecv.at[rows(dp, slab)], s_d2, r_d2, dp=owner)

    loop(0, owners, to_owner)

    @pl.when(active)
    def _():
        drecv[rows(dp, slab), :] = dsend[my_k]
        for copy in late:
            copy.wait()
        drain(drecv.at[pl.ds(0, (n_dp - 1) * slab)], r_d2)
        blocks = [
            jnp.concatenate(
                [drecv[pl.ds(s * parts + p, n_dp, stride=slab), :] for p in range(parts)], axis=1)
            for s in range(cap)]
        results = precondition(
            blocks, [left_buf[s] for s in range(cap)], [right_prev[s] for s in range(cap)])
        for s in range(cap):
            for p in range(parts):
                for q in range(2 * ny):
                    fsend[pl.ds((q // 2) * half * pair + (q % 2) * slab + s * parts + p, half, stride=pair), :] = (
                        results[s][q * half:(q + 1) * half, p * LANES:(p + 1) * LANES])

        def home_rows(yy, zz):
            return rows(yy * half + lax.rem(zz, half), pair)

        def to_home(i):
            yy, zz = y_of(lax.rem(i, ny)), z_of(far_first(i // ny + 1))
            send(fsend.at[home_rows(yy, zz)], frecv.at[rows(my_k, pair)], s_f1, r_f1, dp=yy * nz + zz)

        loop(0, (nz - 1) * ny, to_home)

        def to_column(d):
            send(fsend.at[home_rows(y_of(d), z)], frecv.at[rows(my_k, pair)], s_f1, r_f1,
                 dp=y_of(d) * nz + z)

        loop(1, ny, to_column)
        frecv[rows(my_k, pair), :] = fsend[home_rows(y, z), :]
        drain(frecv.at[pl.ds(0, (owners - 1) * pair)], r_f1)

    @pl.when(jnp.logical_not(active))
    def _():
        drain(frecv, r_f1)

    fb[...] = frecv[...].astype(BF16)
    fmp[mp] = fb[...]
    loop(1, n_mp, lambda d: send(fb, fmp.at[mp], s_f2, r_f2, mp=mp_peer(d)))
    drain(fmp.at[pl.ds(0, n_mp - 1)], r_f2)
    fmpf[...] = fmp[...].astype(F32).reshape(fmpf.shape)
    for h in range(2):
        for b in range(nb):
            hrow[h, b * parts:(b + 1) * parts] = fmpf[pl.ds(places[b] + h * slab, parts), :]
    kind = lax.rem(z, half)
    for c in range(chunks):
        for h in range(2):
            if c < whole:
                fin[c, kind, h] = hrow[h, c * tile:(c + 1) * tile].astype(BF16)
            else:
                finr[kind, h] = hrow[h, c * tile:c * tile + rest]
        buf = fin.at[c] if c < whole else finr

        def spread(i):
            up_to = half // 2
            d = jnp.where(i < up_to, up_to - i, nz - (half - 1 - i))
            send(buf.at[kind], buf.at[kind], s_fz.at[c], r_fz.at[c], dp=y * nz + z_of(d))

        loop(0, half - 1, spread)

    def spans(c):
        lo, hi = lanes(c)
        found = []
        if lo < units:
            found.append((out_a, lo, lo, min(hi, units) - lo))
        if hi > units:
            start = max(lo, units)
            found.append((out_b, start, start - units, hi - start))
        return found

    mine_rows = rows(y, rows_y)
    for c in range(chunks):
        if c < whole:
            drain(fin.at[c, pl.ds(0, half - 1)], r_fz.at[c])
            finf[...] = fin[c].astype(F32).reshape(finf.shape)
            for t in range(tile):
                at = (c * tile + t) * LANES
                ystage[:, at:at + LANES] = jnp.concatenate(
                    [finf[pl.ds(h * tile + t, half, stride=2 * tile), :] for h in range(2)],
                    axis=0).astype(BF16)
        else:
            drain(finr.at[pl.ds(0, half - 1)], r_fz.at[c])
            for i in range(half):
                for h in range(2):
                    at = 8 * (h * half + i)
                    finrf[at:at + rest, :] = finr[i, h]
            for t in range(rest):
                at = (c * tile + t) * LANES
                ystage[:, at:at + LANES] = finrf[pl.ds(t, nz, stride=8), :].astype(BF16)
        for j, (out, src, dst, count) in enumerate(spans(c)):
            loop(1, ny, lambda d: send(
                ystage.at[:, pl.ds(src, count)], out.at[mine_rows, pl.ds(dst, count)],
                s_fy.at[2 * c + j], r_fy.at[2 * c + j], dp=y_of(d) * nz + z))
            pltpu.make_async_copy(
                ystage.at[:, pl.ds(src, count)], out.at[mine_rows, pl.ds(dst, count)],
                own_sem.at[2 * c + j]).start()
    for c in range(chunks):
        for j, (out, src, dst, count) in enumerate(spans(c)):
            arrived = out.at[pl.ds(0, rank - rows_y), pl.ds(dst, count)]
            drain(arrived, r_fy.at[2 * c + j])
            drain(arrived, s_fy.at[2 * c + j])
            pltpu.make_async_copy(
                ystage.at[:, pl.ds(src, count)], out.at[mine_rows, pl.ds(dst, count)],
                own_sem.at[2 * c + j]).wait()

    drain(pbuf.at[pl.ds(0, n_mp - 1)], s_a)
    for c in range(chunks):
        lo, hi = lanes(c)
        drain(yrecv.at[:, :, pl.ds(lo, hi - lo)], s_y.at[c])
        if c < whole:
            drain(zrecv.at[c], s_z.at[c])
            drain(fin.at[c, pl.ds(0, half - 1)], s_fz.at[c])
        else:
            drain(rrecv, s_z.at[c])
            drain(finr.at[pl.ds(0, half - 1)], s_fz.at[c])
    drain(mpbuf.at[pl.ds(0, n_mp - 1)], s_d1)
    drain(fmp.at[pl.ds(0, n_mp - 1)], s_f2)

    @pl.when(active)
    def _():
        drain(dsend.at[pl.ds(0, owners - 1)], s_d2)
        drain(fmpf.at[pl.ds(0, (n_dp - 1) * pair)], s_f1)

    @pl.when(jnp.logical_not(active))
    def _():
        drain(dsend, s_d2)


def placing(first_in, second_in, first_out, second_out):
    first_out[...] = first_in[...]
    second_out[...] = second_in[...]


def shards(
    hidden, cotangent, adapter_down, adapter_up, owner_per_block, left_statistics, right_statistics
):
    n_dp, n_mp = lax.axis_size("dp"), lax.axis_size("mp")
    nz = Z_EXTENT
    ny = n_dp // nz
    tok, units = hidden.shape
    features = cotangent.shape[1]
    rank = adapter_down.shape[1]
    nb = owner_per_block.shape[1]
    cap, width = left_statistics.shape[:2]
    parts = width // LANES
    owners = n_dp // n_mp
    tile = BLOCKS_PER_CHUNK * parts
    whole = nb // BLOCKS_PER_CHUNK
    chunks = whole + 1
    rest = (nb - whole * BLOCKS_PER_CHUNK) * parts
    slab = cap * parts
    keep = -(-nb * parts // 8) * 8
    rows_y = rank // ny

    any_space = pl.BlockSpec(memory_space=pl.ANY)
    dma = pltpu.SemaphoreType.DMA
    vmem = pltpu.VMEM
    cfg = (n_dp, n_mp, ny, nz, rank, width, nb, cap)
    shapes = (
        jax.ShapeDtypeStruct((rank, units), BF16),
        jax.ShapeDtypeStruct((rank, features), BF16),
    )
    update_a, update_b = pl.pallas_call(
        functools.partial(kernel, cfg),
        out_shape=shapes,
        in_specs=[pl.BlockSpec(memory_space=pltpu.SMEM)] + [any_space] * 6,
        out_specs=(any_space, any_space),
        scratch_shapes=[
            vmem((tok, units), BF16),
            vmem((tok, features), BF16),
            vmem((rank, units), BF16),
            vmem((rank, features), BF16),
            vmem((cap, rank, rank), F32),
            vmem((cap, width, width), F32),
            vmem((n_mp, 2 * rank, tok), BF16),
            vmem((ny, rows_y, nb * width), BF16),
            vmem((ny - 1, rows_y, nb * width), BF16),
            vmem((whole, nz * tile, LANES), F32),
            vmem((whole, nz, tile, LANES), BF16),
            vmem((whole, nz - 1, tile, LANES), BF16),
            vmem((nz * 8, LANES), F32),
            vmem((nz, rest, LANES), F32),
            vmem((nz - 1, rest, LANES), F32),
            vmem((keep, LANES), F32),
            vmem((n_mp, keep, LANES), F32),
            vmem((owners, slab, LANES), F32),
            vmem((n_dp * slab, LANES), F32),
            vmem((n_dp * slab, LANES), F32),
            vmem((2 * owners * slab, LANES), F32),
            vmem((2 * owners * slab, LANES), BF16),
            vmem((n_mp, 2 * owners * slab, LANES), BF16),
            vmem((2 * n_mp * owners * slab, LANES), F32),
            vmem((2, keep, LANES), F32),
            vmem((whole, nz // 2, 2, tile, LANES), BF16),
            vmem((nz // 2, 2, rest, LANES), F32),
            vmem((nz * tile, LANES), F32),
            vmem((nz * 8, LANES), F32),
            vmem((rows_y, nb * width), BF16),
            dma((10,)), dma((2,)), dma, dma,
            dma((chunks,)), dma((chunks,)), dma((chunks,)), dma((chunks,)),
            dma, dma, dma, dma, dma, dma, dma, dma,
            dma((chunks,)), dma((chunks,)),
            dma((2 * chunks,)), dma((2 * chunks,)), dma((2 * chunks,)),
        ],
        compiler_params=pltpu.CompilerParams(
            collective_id=0, has_side_effects=True, vmem_limit_bytes=58 * 1024 * 1024
        ),
    )(
        owner_per_block, hidden, cotangent, adapter_down.T, adapter_up,
        left_statistics, right_statistics,
    )
    update_a, update_b = pl.pallas_call(
        placing,
        out_shape=shapes,
        in_specs=[pl.BlockSpec(memory_space=vmem)] * 2,
        out_specs=(pl.BlockSpec(memory_space=vmem), pl.BlockSpec(memory_space=vmem)),
        compiler_params=pltpu.CompilerParams(vmem_limit_bytes=58 * 1024 * 1024),
    )(update_a, update_b)
    return update_a.T, update_b


def solution(mesh):
    return jax.shard_map(
        shards,
        mesh=mesh,
        in_specs=(
            P("dp", "mp"),
            P("dp", "mp"),
            P("mp", None),
            P(None, "mp"),
            P(),
            P("dp", None, None),
            P("dp", None, None),
        ),
        out_specs=(P("mp", None), P(None, "mp")),
        check_vma=False,
    )
```

```python
import functools

import jax
import jax.numpy as jnp
from jax import lax
from jax.experimental import pallas as pl
from jax.experimental.pallas import tpu as pltpu
from jax.sharding import PartitionSpec as P

Z_EXTENT = 16
BLOCKS_PER_CHUNK = 4
LANES = 128

ADAPTER_SCALE = 2.0
BETA_STAT = 0.9
EPS_NORM = 1e-06
MESH = pl.DeviceIdType.MESH
BF16 = jnp.bfloat16
F32 = jnp.float32

NN = (((1,), (0,)), ((), ()))
NT = (((1,), (1,)), ((), ()))
TN = (((0,), (0,)), ((), ()))


def split(value):
    high = value.astype(BF16)
    return high, (value - high.astype(F32)).astype(BF16)


def dot3(first, second, dims):
    (fh, fl), (sh, sl) = split(first), split(second)
    return dot1(fh, sh, dims) + (dot1(fl, sh, dims) + dot1(fh, sl, dims))


def dot1(first, second, dims):
    return lax.dot_general(
        first.astype(BF16), second.astype(BF16), dims, preferred_element_type=F32)


def eye(n):
    return (
        lax.broadcasted_iota(jnp.int32, (n, n), 0) == lax.broadcasted_iota(jnp.int32, (n, n), 1)
    ).astype(F32)


def total(value):
    return jnp.sum(jnp.sum(value, axis=0, keepdims=True), axis=1, keepdims=True)


def precondition(blocks, lefts, rights):
    rank, width = blocks[0].shape
    n = range(len(blocks))
    lefts = [BETA_STAT * lefts[i] + (1.0 - BETA_STAT) * dot1(blocks[i], blocks[i], TN) for i in n]
    rights = [BETA_STAT * rights[i] + (1.0 - BETA_STAT) * dot1(blocks[i], blocks[i], NT) for i in n]
    short = [v.astype(BF16) for v in lefts]
    left_z = [5.0 / (2.0 * jnp.sqrt(total(v * v))) for v in lefts]
    right_z = [5.0 / (2.0 * jnp.sqrt(total(v * v))) for v in rights]
    right_m = [right_z[i] * rights[i] for i in n]

    moved = [dot1(blocks[i], short[i], NN) * left_z[i] for i in n]
    small = right_m
    for _ in range(4):
        moved = [(5.0 * moved[i] - dot1(moved[i], short[i], NN) * left_z[i]) / 4.0 for i in n]
        small = [(5.0 * small[i] - dot1(right_m[i], small[i], NN)) / 4.0 for i in n]
    outs = [(5.0 * blocks[i] - moved[i]) / 4.0 for i in n]
    roots = [(5.0 * eye(rank) - small[i]) / 4.0 for i in n]
    outs = [(5.0 * outs[i] - dot1(outs[i], short[i], NN) * left_z[i]) / 4.0 for i in n]
    roots = [(5.0 * roots[i] - dot1(right_m[i], roots[i], NN)) / 4.0 for i in n]
    gains = [jnp.sqrt(jnp.sqrt(left_z[i])) * jnp.sqrt(jnp.sqrt(right_z[i])) for i in n]
    outs = [dot3(roots[i], outs[i], NN) * gains[i] for i in n]
    return [v * lax.rsqrt(total(v * v) / (rank * width) + EPS_NORM) for v in outs]


def kernel(
    cfg,
    owner_ref, hid_hbm, cot_hbm, down_hbm, up_hbm, left_hbm, right_hbm,
    out_a, out_b,
    hid, cot, down, up, right_prev, left_buf, pbuf, gsend, yrecv, zstage, zsend, zrecv,
    rstage, rsend, rrecv, grow, growb, mpbuf, mpf, dsend, drecv, fsend, frecv, fb, fmp, fmpf, hrow,
    fin, finr, finf, finrf, ystage,
    in_sem, left_sem, s_a, r_a, s_y, r_y, s_z, r_z, s_d1, r_d1, s_d2, r_d2,
    s_f1, r_f1, s_f2, r_f2, s_fz, r_fz, s_fy, r_fy, own_sem,
):
    n_dp, n_mp, ny, nz, rank, width, nb, cap = cfg
    parts = width // LANES
    owners = n_dp // n_mp
    tile = BLOCKS_PER_CHUNK * parts
    whole = nb // BLOCKS_PER_CHUNK
    chunks = whole + 1
    rest = (nb - whole * BLOCKS_PER_CHUNK) * parts
    keep = -(-nb * parts // 8) * 8
    sizes = [tile] * whole + [rest]
    tok, units = hid.shape
    slab = cap * parts
    half = nz // 2
    pair = 2 * slab
    rows_y = rank // ny
    blocks_a = units // width

    dp = lax.axis_index("dp")
    mp = lax.axis_index("mp")
    y, z = dp // nz, lax.rem(dp, nz)
    active = lax.rem(dp, n_mp) == mp
    my_k = dp // n_mp
    kind = lax.rem(z, half)

    def mp_peer(d):
        return lax.rem(mp + d, n_mp)

    def y_of(d):
        return lax.rem(y + d, ny)

    def z_of(d):
        return lax.rem(z + d, nz)

    def far_first(d):
        step = d // 2
        return jnp.where(lax.rem(d, 2) == 0, half + step, half - step)

    def near(i):
        up_to = half // 2
        return jnp.where(i < up_to, up_to - i, nz - (half - 1 - i))

    def send(src, dst, ssem, rsem, **device):
        pltpu.make_async_remote_copy(
            src_ref=src, dst_ref=dst, send_sem=ssem, recv_sem=rsem,
            device_id=device, device_id_type=MESH,
        ).start()

    def drain(ref, sem):
        pltpu.make_async_copy(ref, ref, sem).wait()

    def loop(lower, upper, body):
        def step(i, carry):
            body(i)
            return carry
        lax.fori_loop(lower, upper, step, 0)

    def rows(index, count):
        return pl.ds(pl.multiple_of(index * count, count), count)

    cuts = 4 if units % (4 * LANES) == 0 else 1
    span_in = units // cuts
    loads = []
    for i in range(cuts):
        at = pl.ds(i * span_in, span_in)
        loads.append(pltpu.make_async_copy(hid_hbm.at[:, at], hid.at[:, at], in_sem.at[2 * i]))
        loads.append(pltpu.make_async_copy(down_hbm.at[:, at], down.at[:, at], in_sem.at[2 * i + 1]))
    loads.append(pltpu.make_async_copy(cot_hbm, cot, in_sem.at[2 * cuts]))
    loads.append(pltpu.make_async_copy(up_hbm, up, in_sem.at[2 * cuts + 1]))
    for copy in loads:
        copy.start()
    late = [
        pltpu.make_async_copy(left_hbm, left_buf, left_sem.at[0]),
        pltpu.make_async_copy(right_hbm, right_prev, left_sem.at[1]),
    ]

    barrier = pltpu.get_barrier_semaphore()

    def greet(**device):
        pl.semaphore_signal(barrier, inc=1, device_id=device, device_id_type=MESH)

    loop(1, nz, lambda d: greet(dp=y * nz + z_of(far_first(d))))
    loop(1, n_mp, lambda d: greet(mp=mp_peer(d)))
    loop(1, ny, lambda d: greet(dp=y_of(d) * nz + z))

    acc = jnp.zeros((rank, tok), F32)
    for i in range(cuts):
        loads[2 * i].wait()
        loads[2 * i + 1].wait()
        at = pl.ds(i * span_in, span_in)
        acc = acc + dot1(down[:, at], hid[:, at], NT)
    pbuf[mp, :rank] = acc.astype(BF16)
    loads[-2].wait()
    loads[-1].wait()
    pbuf[mp, rank:] = dot1(up[...], cot[...], NT).astype(BF16)

    pl.semaphore_wait(barrier, (n_mp - 1) + (ny - 1) + (nz - 1))

    loop(1, n_mp, lambda d: send(pbuf.at[mp], pbuf.at[mp], s_a, r_a, mp=mp_peer(d)))

    @pl.when(active)
    def _():
        for copy in late:
            copy.start()

    drain(pbuf.at[pl.ds(0, n_mp - 1)], r_a)
    acc = pbuf[0].astype(F32)
    for d in range(1, n_mp):
        acc = acc + pbuf[d].astype(F32)
    inner_t, outer_t = acc[:rank].astype(BF16), acc[rank:].astype(BF16)

    def lanes(c):
        return c * tile * LANES, c * tile * LANES + sizes[c] * LANES

    for c in range(chunks):
        lo, hi = lanes(c)
        for at in range(lo, hi, width):
            if at < units:
                piece = dot1(outer_t, hid[:, at:at + width], NN)
            else:
                piece = dot1(inner_t, cot[:, at - units:at - units + width], NN)
            gsend[:, :, at:at + width] = piece.astype(BF16).reshape(ny, rows_y, width)
        span = pl.ds(lo, hi - lo)
        loop(1, ny, lambda d: send(
            gsend.at[y_of(d), :, span], yrecv.at[d - 1, :, span],
            s_y.at[c], r_y.at[c], dp=y_of(d) * nz + z))

    groups = n_mp
    mine = [owner_ref[mp, b] for b in range(nb)]
    zero = jnp.int32(0)

    def scan(i, carry):
        first, second, slot = carry
        g = groups * nb - 1 - i
        value = owner_ref[g // nb, lax.rem(g, nb)]
        hits = [value == k * n_mp + mp for k in range(owners)]
        second = tuple(jnp.where(h, f, s) for h, f, s in zip(hits, first, second))
        first = tuple(jnp.where(h, g, f) for h, f in zip(hits, first))
        slot = tuple(
            v + jnp.where(value == mine[b], jnp.where(g < mp * nb + b, 1, 0), 0)
            for b, v in enumerate(slot))
        return first, second, slot

    first, second, slot = lax.fori_loop(
        0, groups * nb, scan, ((zero,) * owners, (zero,) * owners, (zero,) * nb))
    places = [
        lax.rem(mine[b], n_mp) * (owners * pair) + (mine[b] // n_mp) * pair + slot[b] * parts
        for b in range(nb)]

    scale = ADAPTER_SCALE / (tok * n_dp)
    for c in range(chunks):
        lo, hi = lanes(c)
        drain(yrecv.at[:, :, pl.ds(lo, hi - lo)], r_y.at[c])
        acc = gsend[y, :, lo:hi].astype(F32)
        for d in range(ny - 1):
            acc = acc + yrecv[d, :, lo:hi].astype(F32)
        if c < whole:
            for t in range(tile):
                for h in range(2):
                    zstage[c, pl.ds(h * tile + t, half, stride=2 * tile), :] = (
                        acc[h * half:(h + 1) * half, t * LANES:(t + 1) * LANES])
            zsend[c] = zstage[c].reshape(half, 2, tile, LANES).astype(BF16)
            src, dst = zsend.at[c], zrecv.at[c]
        else:
            for t in range(rest):
                rstage[pl.ds(t, nz, stride=8), :] = acc[:, t * LANES:(t + 1) * LANES]
            for i in range(nz):
                rsend[i % half, i // half] = rstage[8 * i:8 * i + rest, :]
            src, dst = rsend, rrecv

        def scatter(i):
            home = z_of(near(i))
            send(src.at[lax.rem(home, half)], dst.at[i], s_z.at[c], r_z.at[c], dp=y * nz + home)

        loop(0, half - 1, scatter)
    for c in range(chunks):
        if c < whole:
            drain(zrecv.at[c], r_z.at[c])
            others = jnp.sum(zrecv[c].astype(F32), axis=0)
            for h in range(2):
                acc = zstage[c, rows(2 * kind + h, tile), :] + others[h]
                grow[h * keep + c * tile:h * keep + (c + 1) * tile] = acc * scale
        else:
            drain(rrecv, r_z.at[c])
            acc = (rsend[kind] + jnp.sum(rrecv[...], axis=0)) * scale
            for h in range(2):
                grow[h * keep + c * tile:h * keep + c * tile + rest] = acc[h]
                used = c * tile + rest
                if keep > used:
                    grow[h * keep + used:(h + 1) * keep] = jnp.zeros((keep - used, LANES), F32)

    growb[...] = grow[...].astype(BF16)
    mpbuf[mp] = growb[...]
    loop(1, n_mp, lambda d: send(growb, mpbuf.at[mp], s_d1, r_d1, mp=mp_peer(d)))
    drain(mpbuf.at[pl.ds(0, n_mp - 1)], r_d1)
    mpf[...] = mpbuf[...].astype(F32)
    for k in range(owners):
        for s, g in enumerate((first[k], second[k])):
            for h in range(2):
                dsend[k, h * slab + s * parts:h * slab + (s + 1) * parts] = mpf[
                    g // nb, pl.ds(h * keep + lax.rem(g, nb) * parts, parts), :]

    def to_owner(k):
        owner = k * n_mp + mp

        @pl.when(owner != dp)
        def _():
            send(dsend.at[k], drecv.at[rows(dp, pair)], s_d2, r_d2, dp=owner)

    loop(0, owners, to_owner)

    @pl.when(active)
    def _():
        drecv[rows(dp, pair), :] = dsend[my_k]
        for copy in late:
            copy.wait()
        drain(drecv.at[pl.ds(0, (n_dp - 1) * pair)], r_d2)

        def part_of(s, p, q):
            at = (q // 2) * nz * pair + (q % 2) * slab + s * parts + p
            return (drecv[pl.ds(at, half, stride=pair), :]
                    + drecv[pl.ds(at + half * pair, half, stride=pair), :])

        blocks = [
            jnp.concatenate(
                [jnp.concatenate([part_of(s, p, q) for q in range(2 * ny)], axis=0)
                 for p in range(parts)], axis=1)
            for s in range(cap)]
        results = precondition(
            blocks, [left_buf[s] for s in range(cap)], [right_prev[s] for s in range(cap)])
        for s in range(cap):
            for p in range(parts):
                for q in range(2 * ny):
                    fsend[pl.ds((q // 2) * half * pair + (q % 2) * slab + s * parts + p, half, stride=pair), :] = (
                        results[s][q * half:(q + 1) * half, p * LANES:(p + 1) * LANES])

        def home_rows(yy, zz):
            return rows(yy * half + lax.rem(zz, half), pair)

        def to_home(i):
            yy, zz = y_of(lax.rem(i, ny)), z_of(far_first(i // ny + 1))
            send(fsend.at[home_rows(yy, zz)], frecv.at[rows(my_k, pair)], s_f1, r_f1, dp=yy * nz + zz)

        loop(0, (nz - 1) * ny, to_home)

        def to_column(d):
            send(fsend.at[home_rows(y_of(d), z)], frecv.at[rows(my_k, pair)], s_f1, r_f1,
                 dp=y_of(d) * nz + z)

        loop(1, ny, to_column)
        frecv[rows(my_k, pair), :] = fsend[home_rows(y, z), :]
        drain(frecv.at[pl.ds(0, (owners - 1) * pair)], r_f1)

    @pl.when(jnp.logical_not(active))
    def _():
        drain(frecv, r_f1)

    fb[...] = frecv[...].astype(BF16)
    fmp[mp] = fb[...]
    loop(1, n_mp, lambda d: send(fb, fmp.at[mp], s_f2, r_f2, mp=mp_peer(d)))
    drain(fmp.at[pl.ds(0, n_mp - 1)], r_f2)
    fmpf[...] = fmp[...].astype(F32).reshape(fmpf.shape)
    for h in range(2):
        for b in range(nb):
            hrow[h, b * parts:(b + 1) * parts] = fmpf[pl.ds(places[b] + h * slab, parts), :]
    for c in range(chunks):
        for h in range(2):
            if c < whole:
                fin[c, kind, h] = hrow[h, c * tile:(c + 1) * tile].astype(BF16)
            else:
                finr[kind, h] = hrow[h, c * tile:c * tile + rest]
        buf = fin.at[c] if c < whole else finr

        def spread(i):
            send(buf.at[kind], buf.at[kind], s_fz.at[c], r_fz.at[c], dp=y * nz + z_of(near(i)))

        loop(0, half - 1, spread)

    def spans(c):
        lo, hi = lanes(c)
        found = []
        if lo < units:
            found.append((out_a, lo, lo, min(hi, units) - lo))
        if hi > units:
            start = max(lo, units)
            found.append((out_b, start, start - units, hi - start))
        return found

    mine_rows = rows(y, rows_y)
    for c in range(chunks):
        if c < whole:
            drain(fin.at[c, pl.ds(0, half - 1)], r_fz.at[c])
            finf[...] = fin[c].astype(F32).reshape(finf.shape)
            for t in range(tile):
                at = (c * tile + t) * LANES
                ystage[:, at:at + LANES] = jnp.concatenate(
                    [finf[pl.ds(h * tile + t, half, stride=2 * tile), :] for h in range(2)],
                    axis=0).astype(BF16)
        else:
            drain(finr.at[pl.ds(0, half - 1)], r_fz.at[c])
            for i in range(half):
                for h in range(2):
                    at = 8 * (h * half + i)
                    finrf[at:at + rest, :] = finr[i, h]
            for t in range(rest):
                at = (c * tile + t) * LANES
                ystage[:, at:at + LANES] = finrf[pl.ds(t, nz, stride=8), :].astype(BF16)
        for j, (out, src, dst, count) in enumerate(spans(c)):
            loop(1, ny, lambda d: send(
                ystage.at[:, pl.ds(src, count)], out.at[mine_rows, pl.ds(dst, count)],
                s_fy.at[2 * c + j], r_fy.at[2 * c + j], dp=y_of(d) * nz + z))
            pltpu.make_async_copy(
                ystage.at[:, pl.ds(src, count)], out.at[mine_rows, pl.ds(dst, count)],
                own_sem.at[2 * c + j]).start()
    for c in range(chunks):
        for j, (out, src, dst, count) in enumerate(spans(c)):
            arrived = out.at[pl.ds(0, rank - rows_y), pl.ds(dst, count)]
            drain(arrived, r_fy.at[2 * c + j])
            drain(arrived, s_fy.at[2 * c + j])
            pltpu.make_async_copy(
                ystage.at[:, pl.ds(src, count)], out.at[mine_rows, pl.ds(dst, count)],
                own_sem.at[2 * c + j]).wait()

    drain(pbuf.at[pl.ds(0, n_mp - 1)], s_a)
    for c in range(chunks):
        lo, hi = lanes(c)
        drain(yrecv.at[:, :, pl.ds(lo, hi - lo)], s_y.at[c])
        if c < whole:
            drain(zrecv.at[c], s_z.at[c])
            drain(fin.at[c, pl.ds(0, half - 1)], s_fz.at[c])
        else:
            drain(rrecv, s_z.at[c])
            drain(finr.at[pl.ds(0, half - 1)], s_fz.at[c])
    drain(mpbuf.at[pl.ds(0, n_mp - 1)], s_d1)
    drain(fmp.at[pl.ds(0, n_mp - 1)], s_f2)

    @pl.when(active)
    def _():
        drain(dsend.at[pl.ds(0, owners - 1)], s_d2)
        drain(fmpf.at[pl.ds(0, (n_dp - 1) * pair)], s_f1)

    @pl.when(jnp.logical_not(active))
    def _():
        drain(dsend, s_d2)


def placing(first_in, second_in, first_out, second_out):
    first_out[...] = first_in[...]
    second_out[...] = second_in[...]


def shards(
    hidden, cotangent, adapter_down, adapter_up, owner_per_block, left_statistics, right_statistics
):
    n_dp, n_mp = lax.axis_size("dp"), lax.axis_size("mp")
    nz = Z_EXTENT
    ny = n_dp // nz
    tok, units = hidden.shape
    features = cotangent.shape[1]
    rank = adapter_down.shape[1]
    nb = owner_per_block.shape[1]
    cap, width = left_statistics.shape[:2]
    parts = width // LANES
    owners = n_dp // n_mp
    tile = BLOCKS_PER_CHUNK * parts
    whole = nb // BLOCKS_PER_CHUNK
    chunks = whole + 1
    rest = (nb - whole * BLOCKS_PER_CHUNK) * parts
    slab = cap * parts
    keep = -(-nb * parts // 8) * 8
    rows_y = rank // ny

    any_space = pl.BlockSpec(memory_space=pl.ANY)
    dma = pltpu.SemaphoreType.DMA
    vmem = pltpu.VMEM
    cfg = (n_dp, n_mp, ny, nz, rank, width, nb, cap)
    shapes = (
        jax.ShapeDtypeStruct((rank, units), BF16),
        jax.ShapeDtypeStruct((rank, features), BF16),
    )
    update_a, update_b = pl.pallas_call(
        functools.partial(kernel, cfg),
        out_shape=shapes,
        in_specs=[pl.BlockSpec(memory_space=pltpu.SMEM)] + [any_space] * 6,
        out_specs=(any_space, any_space),
        scratch_shapes=[
            vmem((tok, units), BF16),
            vmem((tok, features), BF16),
            vmem((rank, units), BF16),
            vmem((rank, features), BF16),
            vmem((cap, rank, rank), F32),
            vmem((cap, width, width), F32),
            vmem((n_mp, 2 * rank, tok), BF16),
            vmem((ny, rows_y, nb * width), BF16),
            vmem((ny - 1, rows_y, nb * width), BF16),
            vmem((whole, nz * tile, LANES), F32),
            vmem((whole, nz // 2, 2, tile, LANES), BF16),
            vmem((whole, nz // 2 - 1, 2, tile, LANES), BF16),
            vmem((nz * 8, LANES), F32),
            vmem((nz // 2, 2, rest, LANES), F32),
            vmem((nz // 2 - 1, 2, rest, LANES), F32),
            vmem((2 * keep, LANES), F32),
            vmem((2 * keep, LANES), BF16),
            vmem((n_mp, 2 * keep, LANES), BF16),
            vmem((n_mp, 2 * keep, LANES), F32),
            vmem((owners, 2 * slab, LANES), F32),
            vmem((2 * n_dp * slab, LANES), F32),
            vmem((n_dp * slab, LANES), F32),
            vmem((2 * owners * slab, LANES), F32),
            vmem((2 * owners * slab, LANES), BF16),
            vmem((n_mp, 2 * owners * slab, LANES), BF16),
            vmem((2 * n_mp * owners * slab, LANES), F32),
            vmem((2, keep, LANES), F32),
            vmem((whole, nz // 2, 2, tile, LANES), BF16),
            vmem((nz // 2, 2, rest, LANES), F32),
            vmem((nz * tile, LANES), F32),
            vmem((nz * 8, LANES), F32),
            vmem((rows_y, nb * width), BF16),
            dma((10,)), dma((2,)), dma, dma,
            dma((chunks,)), dma((chunks,)), dma((chunks,)), dma((chunks,)),
            dma, dma, dma, dma, dma, dma, dma, dma,
            dma((chunks,)), dma((chunks,)),
            dma((2 * chunks,)), dma((2 * chunks,)), dma((2 * chunks,)),
        ],
        compiler_params=pltpu.CompilerParams(
            collective_id=0, has_side_effects=True, vmem_limit_bytes=58 * 1024 * 1024
        ),
    )(
        owner_per_block, hidden, cotangent, adapter_down.T, adapter_up,
        left_statistics, right_statistics,
    )
    update_a, update_b = pl.pallas_call(
        placing,
        out_shape=shapes,
        in_specs=[pl.BlockSpec(memory_space=vmem)] * 2,
        out_specs=(pl.BlockSpec(memory_space=vmem), pl.BlockSpec(memory_space=vmem)),
        compiler_params=pltpu.CompilerParams(vmem_limit_bytes=58 * 1024 * 1024),
    )(update_a, update_b)
    return update_a.T, update_b


def solution(mesh):
    return jax.shard_map(
        shards,
        mesh=mesh,
        in_specs=(
            P("dp", "mp"),
            P("dp", "mp"),
            P("mp", None),
            P(None, "mp"),
            P(),
            P("dp", None, None),
            P("dp", None, None),
        ),
        out_specs=(P("mp", None), P(None, "mp")),
        check_vma=False,
    )
```

```python
import functools

import jax
import jax.numpy as jnp
from jax import lax
from jax.experimental import pallas as pl
from jax.experimental.pallas import tpu as pltpu
from jax.sharding import PartitionSpec as P

Z_EXTENT = 16
BLOCKS_PER_CHUNK = 4
LANES = 128

ADAPTER_SCALE = 2.0
BETA_STAT = 0.9
EPS_NORM = 1e-06
MESH = pl.DeviceIdType.MESH
BF16 = jnp.bfloat16
F32 = jnp.float32

NN = (((1,), (0,)), ((), ()))
NT = (((1,), (1,)), ((), ()))
TN = (((0,), (0,)), ((), ()))


def split(value):
    high = value.astype(BF16)
    return high, (value - high.astype(F32)).astype(BF16)


def dot3(first, second, dims):
    (fh, fl), (sh, sl) = split(first), split(second)
    return dot1(fh, sh, dims) + (dot1(fl, sh, dims) + dot1(fh, sl, dims))


def dot1(first, second, dims):
    return lax.dot_general(
        first.astype(BF16), second.astype(BF16), dims, preferred_element_type=F32)


def eye(n):
    return (
        lax.broadcasted_iota(jnp.int32, (n, n), 0) == lax.broadcasted_iota(jnp.int32, (n, n), 1)
    ).astype(F32)


def total(value):
    return jnp.sum(jnp.sum(value, axis=0, keepdims=True), axis=1, keepdims=True)


def precondition(blocks, lefts, rights):
    rank, width = blocks[0].shape
    n = range(len(blocks))
    lefts = [BETA_STAT * lefts[i] + (1.0 - BETA_STAT) * dot1(blocks[i], blocks[i], TN) for i in n]
    rights = [BETA_STAT * rights[i] + (1.0 - BETA_STAT) * dot1(blocks[i], blocks[i], NT) for i in n]
    short = [v.astype(BF16) for v in lefts]
    left_z = [5.0 / (2.0 * jnp.sqrt(total(v * v))) for v in lefts]
    right_z = [5.0 / (2.0 * jnp.sqrt(total(v * v))) for v in rights]
    right_m = [right_z[i] * rights[i] for i in n]

    moved = [dot1(blocks[i], short[i], NN) * left_z[i] for i in n]
    small = right_m
    for _ in range(4):
        moved = [(5.0 * moved[i] - dot1(moved[i], short[i], NN) * left_z[i]) / 4.0 for i in n]
        small = [(5.0 * small[i] - dot1(right_m[i], small[i], NN)) / 4.0 for i in n]
    outs = [(5.0 * blocks[i] - moved[i]) / 4.0 for i in n]
    roots = [(5.0 * eye(rank) - small[i]) / 4.0 for i in n]
    outs = [(5.0 * outs[i] - dot1(outs[i], short[i], NN) * left_z[i]) / 4.0 for i in n]
    roots = [(5.0 * roots[i] - dot1(right_m[i], roots[i], NN)) / 4.0 for i in n]
    gains = [jnp.sqrt(jnp.sqrt(left_z[i])) * jnp.sqrt(jnp.sqrt(right_z[i])) for i in n]
    outs = [dot3(roots[i], outs[i], NN) * gains[i] for i in n]
    return [v * lax.rsqrt(total(v * v) / (rank * width) + EPS_NORM) for v in outs]


def kernel(
    cfg,
    owner_ref, hid_hbm, cot_hbm, down_hbm, up_hbm, left_hbm, right_hbm,
    out_a, out_b,
    hid, cot, down, up, right_prev, left_buf, pbuf, gsend, yrecv, zstage, zsend, zrecv,
    rstage, rsend, rrecv, grow, growb, mpbuf, mpf, dsend, drecv, fsend, frecv, fb, fmp, fmpf, hrow,
    fin, finr, finf, finrf, ystage,
    in_sem, left_sem, s_a, r_a, s_y, r_y, s_z, r_z, s_d1, r_d1, s_d2, r_d2,
    s_f1, r_f1, s_f2, r_f2, s_fz, r_fz, s_fy, r_fy, own_sem,
):
    n_dp, n_mp, ny, nz, rank, width, nb, cap = cfg
    parts = width // LANES
    owners = n_dp // n_mp
    tile = BLOCKS_PER_CHUNK * parts
    whole = nb // BLOCKS_PER_CHUNK
    chunks = whole + 1
    rest = (nb - whole * BLOCKS_PER_CHUNK) * parts
    keep = -(-nb * parts // 8) * 8
    sizes = [tile] * whole + [rest]
    tok, units = hid.shape
    slab = cap * parts
    half = nz // 2
    pair = 2 * slab
    rows_y = rank // ny
    blocks_a = units // width

    dp = lax.axis_index("dp")
    mp = lax.axis_index("mp")
    y, z = dp // nz, lax.rem(dp, nz)
    active = lax.rem(dp, n_mp) == mp
    my_k = dp // n_mp
    kind = lax.rem(z, half)

    def mp_peer(d):
        return lax.rem(mp + d, n_mp)

    def y_of(d):
        return lax.rem(y + d, ny)

    def z_of(d):
        return lax.rem(z + d, nz)

    def far_first(d):
        step = d // 2
        return jnp.where(lax.rem(d, 2) == 0, half + step, half - step)

    def near(i):
        up_to = half // 2
        return jnp.where(i < up_to, up_to - i, nz - (half - 1 - i))

    def send(src, dst, ssem, rsem, **device):
        pltpu.make_async_remote_copy(
            src_ref=src, dst_ref=dst, send_sem=ssem, recv_sem=rsem,
            device_id=device, device_id_type=MESH,
        ).start()

    def drain(ref, sem):
        pltpu.make_async_copy(ref, ref, sem).wait()

    def loop(lower, upper, body):
        def step(i, carry):
            body(i)
            return carry
        lax.fori_loop(lower, upper, step, 0)

    def rows(index, count):
        return pl.ds(pl.multiple_of(index * count, count), count)

    cuts = 4 if units % (4 * LANES) == 0 else 1
    span_in = units // cuts
    loads = []
    for i in range(cuts):
        at = pl.ds(i * span_in, span_in)
        loads.append(pltpu.make_async_copy(hid_hbm.at[:, at], hid.at[:, at], in_sem.at[2 * i]))
        loads.append(pltpu.make_async_copy(down_hbm.at[:, at], down.at[:, at], in_sem.at[2 * i + 1]))
    loads.append(pltpu.make_async_copy(cot_hbm, cot, in_sem.at[2 * cuts]))
    loads.append(pltpu.make_async_copy(up_hbm, up, in_sem.at[2 * cuts + 1]))
    for copy in loads:
        copy.start()
    late = [
        pltpu.make_async_copy(left_hbm, left_buf, left_sem.at[0]),
        pltpu.make_async_copy(right_hbm, right_prev, left_sem.at[1]),
    ]

    barrier = pltpu.get_barrier_semaphore()

    def greet(**device):
        pl.semaphore_signal(barrier, inc=1, device_id=device, device_id_type=MESH)

    loop(1, nz, lambda d: greet(dp=y * nz + z_of(far_first(d))))
    loop(1, n_mp, lambda d: greet(mp=mp_peer(d)))
    loop(1, ny, lambda d: greet(dp=y_of(d) * nz + z))

    acc = jnp.zeros((rank, tok), F32)
    for i in range(cuts):
        loads[2 * i].wait()
        loads[2 * i + 1].wait()
        at = pl.ds(i * span_in, span_in)
        acc = acc + dot1(down[:, at], hid[:, at], NT)
    pbuf[mp, :rank] = acc.astype(BF16)
    loads[-2].wait()
    loads[-1].wait()
    pbuf[mp, rank:] = dot1(up[...], cot[...], NT).astype(BF16)

    pl.semaphore_wait(barrier, (n_mp - 1) + (ny - 1) + (nz - 1))

    loop(1, n_mp, lambda d: send(pbuf.at[mp], pbuf.at[mp], s_a, r_a, mp=mp_peer(d)))

    @pl.when(active)
    def _():
        for copy in late:
            copy.start()

    drain(pbuf.at[pl.ds(0, n_mp - 1)], r_a)
    acc = pbuf[0].astype(F32)
    for d in range(1, n_mp):
        acc = acc + pbuf[d].astype(F32)
    inner_t, outer_t = acc[:rank].astype(BF16), acc[rank:].astype(BF16)

    def lanes(c):
        return c * tile * LANES, c * tile * LANES + sizes[c] * LANES

    for c in [chunks - 1] + list(range(whole)):
        lo, hi = lanes(c)
        for at in range(lo, hi, width):
            if at < units:
                piece = dot1(outer_t, hid[:, at:at + width], NN)
            else:
                piece = dot1(inner_t, cot[:, at - units:at - units + width], NN)
            gsend[:, :, at:at + width] = piece.astype(BF16).reshape(ny, rows_y, width)
        span = pl.ds(lo, hi - lo)
        loop(1, ny, lambda d: send(
            gsend.at[y_of(d), :, span], yrecv.at[d - 1, :, span],
            s_y.at[c], r_y.at[c], dp=y_of(d) * nz + z))

    groups = n_mp
    mine = [owner_ref[mp, b] for b in range(nb)]
    zero = jnp.int32(0)

    def scan(i, carry):
        first, second, slot = carry
        g = groups * nb - 1 - i
        value = owner_ref[g // nb, lax.rem(g, nb)]
        hits = [value == k * n_mp + mp for k in range(owners)]
        second = tuple(jnp.where(h, f, s) for h, f, s in zip(hits, first, second))
        first = tuple(jnp.where(h, g, f) for h, f in zip(hits, first))
        slot = tuple(
            v + jnp.where(value == mine[b], jnp.where(g < mp * nb + b, 1, 0), 0)
            for b, v in enumerate(slot))
        return first, second, slot

    first, second, slot = lax.fori_loop(
        0, groups * nb, scan, ((zero,) * owners, (zero,) * owners, (zero,) * nb))
    places = [
        lax.rem(mine[b], n_mp) * (owners * pair) + (mine[b] // n_mp) * pair + slot[b] * parts
        for b in range(nb)]

    scale = ADAPTER_SCALE / (tok * n_dp)
    for c in [chunks - 1] + list(range(whole)):
        lo, hi = lanes(c)
        drain(yrecv.at[:, :, pl.ds(lo, hi - lo)], r_y.at[c])
        acc = gsend[y, :, lo:hi].astype(F32)
        for d in range(ny - 1):
            acc = acc + yrecv[d, :, lo:hi].astype(F32)
        if c < whole:
            for t in range(tile):
                for h in range(2):
                    zstage[c, pl.ds(h * tile + t, half, stride=2 * tile), :] = (
                        acc[h * half:(h + 1) * half, t * LANES:(t + 1) * LANES])
            zsend[c] = zstage[c].reshape(half, 2, tile, LANES).astype(BF16)
            src, dst = zsend.at[c], zrecv.at[c]
        else:
            for t in range(rest):
                rstage[pl.ds(t, nz, stride=8), :] = acc[:, t * LANES:(t + 1) * LANES]
            for i in range(nz):
                rsend[i % half, i // half] = rstage[8 * i:8 * i + rest, :]
            src, dst = rsend, rrecv

        def scatter(i):
            home = z_of(near(i))
            send(src.at[lax.rem(home, half)], dst.at[i], s_z.at[c], r_z.at[c], dp=y * nz + home)

        loop(0, half - 1, scatter)
    for c in [chunks - 1] + list(range(whole)):
        if c < whole:
            drain(zrecv.at[c], r_z.at[c])
            others = jnp.sum(zrecv[c].astype(F32), axis=0)
            for h in range(2):
                acc = zstage[c, rows(2 * kind + h, tile), :] + others[h]
                grow[h * keep + c * tile:h * keep + (c + 1) * tile] = acc * scale
        else:
            drain(rrecv, r_z.at[c])
            acc = (rsend[kind] + jnp.sum(rrecv[...], axis=0)) * scale
            for h in range(2):
                grow[h * keep + c * tile:h * keep + c * tile + rest] = acc[h]
                used = c * tile + rest
                if keep > used:
                    grow[h * keep + used:(h + 1) * keep] = jnp.zeros((keep - used, LANES), F32)

    growb[...] = grow[...].astype(BF16)
    mpbuf[mp] = growb[...]
    loop(1, n_mp, lambda d: send(growb, mpbuf.at[mp], s_d1, r_d1, mp=mp_peer(d)))
    drain(mpbuf.at[pl.ds(0, n_mp - 1)], r_d1)
    mpf[...] = mpbuf[...].astype(F32)
    for k in range(owners):
        for s, g in enumerate((first[k], second[k])):
            for h in range(2):
                dsend[k, h * slab + s * parts:h * slab + (s + 1) * parts] = mpf[
                    g // nb, pl.ds(h * keep + lax.rem(g, nb) * parts, parts), :]

    def to_owner(k):
        owner = k * n_mp + mp

        @pl.when(owner != dp)
        def _():
            send(dsend.at[k], drecv.at[rows(dp, pair)], s_d2, r_d2, dp=owner)

    loop(0, owners, to_owner)

    @pl.when(active)
    def _():
        drecv[rows(dp, pair), :] = dsend[my_k]
        for copy in late:
            copy.wait()
        drain(drecv.at[pl.ds(0, (n_dp - 1) * pair)], r_d2)

        def part_of(s, p, q):
            at = (q // 2) * nz * pair + (q % 2) * slab + s * parts + p
            return (drecv[pl.ds(at, half, stride=pair), :]
                    + drecv[pl.ds(at + half * pair, half, stride=pair), :])

        blocks = [
            jnp.concatenate(
                [jnp.concatenate([part_of(s, p, q) for q in range(2 * ny)], axis=0)
                 for p in range(parts)], axis=1)
            for s in range(cap)]
        results = precondition(
            blocks, [left_buf[s] for s in range(cap)], [right_prev[s] for s in range(cap)])
        for s in range(cap):
            for p in range(parts):
                for q in range(2 * ny):
                    fsend[pl.ds((q // 2) * half * pair + (q % 2) * slab + s * parts + p, half, stride=pair), :] = (
                        results[s][q * half:(q + 1) * half, p * LANES:(p + 1) * LANES])

        def home_rows(yy, zz):
            return rows(yy * half + lax.rem(zz, half), pair)

        def to_home(i):
            yy, zz = y_of(lax.rem(i, ny)), z_of(far_first(i // ny + 1))
            send(fsend.at[home_rows(yy, zz)], frecv.at[rows(my_k, pair)], s_f1, r_f1, dp=yy * nz + zz)

        loop(0, (nz - 1) * ny, to_home)

        def to_column(d):
            send(fsend.at[home_rows(y_of(d), z)], frecv.at[rows(my_k, pair)], s_f1, r_f1,
                 dp=y_of(d) * nz + z)

        loop(1, ny, to_column)
        frecv[rows(my_k, pair), :] = fsend[home_rows(y, z), :]
        drain(frecv.at[pl.ds(0, (owners - 1) * pair)], r_f1)

    @pl.when(jnp.logical_not(active))
    def _():
        drain(frecv, r_f1)

    fb[...] = frecv[...].astype(BF16)
    fmp[mp] = fb[...]
    loop(1, n_mp, lambda d: send(fb, fmp.at[mp], s_f2, r_f2, mp=mp_peer(d)))
    drain(fmp.at[pl.ds(0, n_mp - 1)], r_f2)
    fmpf[...] = fmp[...].astype(F32).reshape(fmpf.shape)
    for h in range(2):
        for b in range(nb):
            hrow[h, b * parts:(b + 1) * parts] = fmpf[pl.ds(places[b] + h * slab, parts), :]
    for c in range(chunks):
        for h in range(2):
            if c < whole:
                fin[c, kind, h] = hrow[h, c * tile:(c + 1) * tile].astype(BF16)
            else:
                finr[kind, h] = hrow[h, c * tile:c * tile + rest]
        buf = fin.at[c] if c < whole else finr

        def spread(i):
            send(buf.at[kind], buf.at[kind], s_fz.at[c], r_fz.at[c], dp=y * nz + z_of(near(i)))

        loop(0, half - 1, spread)

    def spans(c):
        lo, hi = lanes(c)
        found = []
        if lo < units:
            found.append((out_a, lo, lo, min(hi, units) - lo))
        if hi > units:
            start = max(lo, units)
            found.append((out_b, start, start - units, hi - start))
        return found

    mine_rows = rows(y, rows_y)
    for c in range(chunks):
        if c < whole:
            drain(fin.at[c, pl.ds(0, half - 1)], r_fz.at[c])
            finf[...] = fin[c].astype(F32).reshape(finf.shape)
            for t in range(tile):
                at = (c * tile + t) * LANES
                ystage[:, at:at + LANES] = jnp.concatenate(
                    [finf[pl.ds(h * tile + t, half, stride=2 * tile), :] for h in range(2)],
                    axis=0).astype(BF16)
        else:
            drain(finr.at[pl.ds(0, half - 1)], r_fz.at[c])
            for i in range(half):
                for h in range(2):
                    at = 8 * (h * half + i)
                    finrf[at:at + rest, :] = finr[i, h]
            for t in range(rest):
                at = (c * tile + t) * LANES
                ystage[:, at:at + LANES] = finrf[pl.ds(t, nz, stride=8), :].astype(BF16)
        for j, (out, src, dst, count) in enumerate(spans(c)):
            loop(1, ny, lambda d: send(
                ystage.at[:, pl.ds(src, count)], out.at[mine_rows, pl.ds(dst, count)],
                s_fy.at[2 * c + j], r_fy.at[2 * c + j], dp=y_of(d) * nz + z))
            pltpu.make_async_copy(
                ystage.at[:, pl.ds(src, count)], out.at[mine_rows, pl.ds(dst, count)],
                own_sem.at[2 * c + j]).start()
    for c in range(chunks):
        for j, (out, src, dst, count) in enumerate(spans(c)):
            arrived = out.at[pl.ds(0, rank - rows_y), pl.ds(dst, count)]
            drain(arrived, r_fy.at[2 * c + j])
            drain(arrived, s_fy.at[2 * c + j])
            pltpu.make_async_copy(
                ystage.at[:, pl.ds(src, count)], out.at[mine_rows, pl.ds(dst, count)],
                own_sem.at[2 * c + j]).wait()

    drain(pbuf.at[pl.ds(0, n_mp - 1)], s_a)
    for c in range(chunks):
        lo, hi = lanes(c)
        drain(yrecv.at[:, :, pl.ds(lo, hi - lo)], s_y.at[c])
        if c < whole:
            drain(zrecv.at[c], s_z.at[c])
            drain(fin.at[c, pl.ds(0, half - 1)], s_fz.at[c])
        else:
            drain(rrecv, s_z.at[c])
            drain(finr.at[pl.ds(0, half - 1)], s_fz.at[c])
    drain(mpbuf.at[pl.ds(0, n_mp - 1)], s_d1)
    drain(fmp.at[pl.ds(0, n_mp - 1)], s_f2)

    @pl.when(active)
    def _():
        drain(dsend.at[pl.ds(0, owners - 1)], s_d2)
        drain(fmpf.at[pl.ds(0, (n_dp - 1) * pair)], s_f1)

    @pl.when(jnp.logical_not(active))
    def _():
        drain(dsend, s_d2)


def placing(first_in, second_in, first_out, second_out, first, second, sem_in, sem_out):
    pieces = []
    for source, held, target in ((first_in, first, first_out), (second_in, second, second_out)):
        step = max(16, source.shape[0] // 4)
        for at in range(0, source.shape[0], step):
            span = pl.ds(at, min(step, source.shape[0] - at))
            pieces.append((source.at[span], held.at[span], target.at[span]))
    inward = [pltpu.make_async_copy(a, b, sem_in.at[i]) for i, (a, b, _) in enumerate(pieces)]
    outward = [pltpu.make_async_copy(b, c, sem_out.at[i]) for i, (_, b, c) in enumerate(pieces)]
    for copy in inward:
        copy.start()
    for first_half, second_half in zip(inward, outward):
        first_half.wait()
        second_half.start()
    for copy in outward:
        copy.wait()


def shards(
    hidden, cotangent, adapter_down, adapter_up, owner_per_block, left_statistics, right_statistics
):
    n_dp, n_mp = lax.axis_size("dp"), lax.axis_size("mp")
    nz = Z_EXTENT
    ny = n_dp // nz
    tok, units = hidden.shape
    features = cotangent.shape[1]
    rank = adapter_down.shape[1]
    nb = owner_per_block.shape[1]
    cap, width = left_statistics.shape[:2]
    parts = width // LANES
    owners = n_dp // n_mp
    tile = BLOCKS_PER_CHUNK * parts
    whole = nb // BLOCKS_PER_CHUNK
    chunks = whole + 1
    rest = (nb - whole * BLOCKS_PER_CHUNK) * parts
    slab = cap * parts
    keep = -(-nb * parts // 8) * 8
    rows_y = rank // ny

    any_space = pl.BlockSpec(memory_space=pl.ANY)
    dma = pltpu.SemaphoreType.DMA
    vmem = pltpu.VMEM
    cfg = (n_dp, n_mp, ny, nz, rank, width, nb, cap)
    shapes = (
        jax.ShapeDtypeStruct((rank, units), BF16),
        jax.ShapeDtypeStruct((rank, features), BF16),
    )
    update_a, update_b = pl.pallas_call(
        functools.partial(kernel, cfg),
        out_shape=shapes,
        in_specs=[pl.BlockSpec(memory_space=pltpu.SMEM)] + [any_space] * 6,
        out_specs=(any_space, any_space),
        scratch_shapes=[
            vmem((tok, units), BF16),
            vmem((tok, features), BF16),
            vmem((rank, units), BF16),
            vmem((rank, features), BF16),
            vmem((cap, rank, rank), F32),
            vmem((cap, width, width), F32),
            vmem((n_mp, 2 * rank, tok), BF16),
            vmem((ny, rows_y, nb * width), BF16),
            vmem((ny - 1, rows_y, nb * width), BF16),
            vmem((whole, nz * tile, LANES), F32),
            vmem((whole, nz // 2, 2, tile, LANES), BF16),
            vmem((whole, nz // 2 - 1, 2, tile, LANES), BF16),
            vmem((nz * 8, LANES), F32),
            vmem((nz // 2, 2, rest, LANES), F32),
            vmem((nz // 2 - 1, 2, rest, LANES), F32),
            vmem((2 * keep, LANES), F32),
            vmem((2 * keep, LANES), BF16),
            vmem((n_mp, 2 * keep, LANES), BF16),
            vmem((n_mp, 2 * keep, LANES), F32),
            vmem((owners, 2 * slab, LANES), F32),
            vmem((2 * n_dp * slab, LANES), F32),
            vmem((n_dp * slab, LANES), F32),
            vmem((2 * owners * slab, LANES), F32),
            vmem((2 * owners * slab, LANES), BF16),
            vmem((n_mp, 2 * owners * slab, LANES), BF16),
            vmem((2 * n_mp * owners * slab, LANES), F32),
            vmem((2, keep, LANES), F32),
            vmem((whole, nz // 2, 2, tile, LANES), BF16),
            vmem((nz // 2, 2, rest, LANES), F32),
            vmem((nz * tile, LANES), F32),
            vmem((nz * 8, LANES), F32),
            vmem((rows_y, nb * width), BF16),
            dma((10,)), dma((2,)), dma, dma,
            dma((chunks,)), dma((chunks,)), dma((chunks,)), dma((chunks,)),
            dma, dma, dma, dma, dma, dma, dma, dma,
            dma((chunks,)), dma((chunks,)),
            dma((2 * chunks,)), dma((2 * chunks,)), dma((2 * chunks,)),
        ],
        compiler_params=pltpu.CompilerParams(
            collective_id=0, has_side_effects=True, vmem_limit_bytes=58 * 1024 * 1024
        ),
    )(
        owner_per_block, hidden, cotangent, adapter_down.T, adapter_up,
        left_statistics, right_statistics,
    )
    update_a, update_b = pl.pallas_call(
        placing,
        out_shape=shapes,
        in_specs=[any_space] * 2,
        out_specs=(any_space, any_space),
        scratch_shapes=[
            vmem((rank, units), BF16), vmem((rank, features), BF16), dma((8,)), dma((8,)),
        ],
        compiler_params=pltpu.CompilerParams(vmem_limit_bytes=58 * 1024 * 1024),
    )(update_a, update_b)
    return update_a.T, update_b


def solution(mesh):
    return jax.shard_map(
        shards,
        mesh=mesh,
        in_specs=(
            P("dp", "mp"),
            P("dp", "mp"),
            P("mp", None),
            P(None, "mp"),
            P(),
            P("dp", None, None),
            P("dp", None, None),
        ),
        out_specs=(P("mp", None), P(None, "mp")),
        check_vma=False,
    )
```
